256 devices in a mesh: tm: 8 (over z_lo, core), height: 32 (over x, y, z_hi).
Axes of the slice: x: 4, y: 4, z: 8 (z_hi: 2, z_lo: 4; z = z_hi * 4 + z_lo), core: 2. Of those that a mesh axis runs over, the one named last changes fastest.
Arguments:
- clean_latents: bfloat16 [32, 128, 16, 3072], P('tm', 'height'), may hold values from -6 to 6
- gaussian_noise: bfloat16 [32, 128, 16, 3072], P('tm', 'height'), may hold values from -6 to 6
- text_states: bfloat16 [256, 3072], replicated, may hold values from -6 to 6
- queries: bfloat16 [32, 128, 16, 1536], P('tm', 'height'), may hold values from -40 to 40
- key_states: bfloat16 [32, 128, 16, 1536], P('tm', 'height'), may hold values from -8 to 8
- cotangent: bfloat16 [32, 128, 16, 1536], P('tm', 'height'), may hold values from -240 to 240
- text_keys: bfloat16 [256, 1536], replicated, may hold values from -6 to 6
- window_radii: int32 [12, 3], replicated, may hold values from 0 to 1
- timestep: int32 [1], replicated, may hold values from 200 to 799
- sketch_seed: int32 [1], replicated, may hold values from 0 to 65535
- down_image: bfloat16 [3072, 16], replicated, may hold values from -0.109375 to 0.109375
- up_image: bfloat16 [16, 1536], replicated, may hold values from -1.5 to 1.5
- down_text: bfloat16 [3072, 16], replicated, may hold values from -0.109375 to 0.109375
- up_text: bfloat16 [16, 1536], replicated, may hold values from -1.5 to 1.5
Outputs:
- value_grad: bfloat16 [32, 128, 16, 1536], P('tm', 'height')
- grad_sketch: float32 [16384], replicated
The draws below stay inside these ranges and needn't reach their ends.
All inputs are finite; a program needn't handle non-finite values.
Results may differ from the reference program's by a relative error of at most 0.0075.
Values may be sent and summed in bfloat16 or wider, within the bound.
A program may use at most 128 MiB of HBM per device.

```python
import jax
import jax.numpy as jnp
from jax import lax

D = 3072
HDIM = 128
TXT = 256
HEADS = 12
RANK = 16
SKETCH = 16384
FT = 4
HR = 4
TW = 8
W = 16
HD = 1536
NF = 32
NR = 128
TOKENS = 65536
PARAMS = 147456
N_TM = 8
N_HEIGHT = 32


def drawn_pair(key):
    query_key = jax.random.fold_in(key, 11)
    key_key = jax.random.fold_in(key, 12)
    shape = (NF, NR, W, HD)
    base_keys = jnp.clip(jax.random.normal(key_key, shape, jnp.float32), -4.0, 4.0)
    base_queries = jnp.clip(jax.random.normal(query_key, shape, jnp.float32), -4.0, 4.0)
    return (base_queries, base_keys)


def draw_queries(key, part):
    return drawn_pair(key)[0].astype(jnp.bfloat16)


def draw_key_states(key, part):
    return drawn_pair(key)[1].astype(jnp.bfloat16)


def with_ends(drawn, stream_key, least, top_value):
    place = [jax.random.randint(jax.random.fold_in(stream_key, axis), (), 0, length) for axis, length in enumerate(drawn.shape)]
    widest = drawn.shape.index(max(drawn.shape))
    neighbour = place[:widest] + [(place[widest] + 1) % drawn.shape[widest]] + place[widest + 1:]
    return drawn.at[tuple(place)].set(least).at[tuple(neighbour)].set(top_value)


def level_of(own_key, extent, split, low, top_value):
    factor_of = 1.0
    for dim, shards_of in split:
        draws = jax.random.uniform(jax.random.fold_in(jax.random.fold_in(own_key, 6), dim), (shards_of,), jnp.float32, low / len(split), top_value / len(split))
        factor_of = factor_of * jnp.repeat(jnp.exp(draws), extent[dim] // shards_of).reshape((-1,) + (1,) * (len(extent) - 1 - dim))
    return factor_of


def noise(rng, extent, deviation, limit, cuts=(), kind=jnp.bfloat16):
    array = deviation * jax.random.normal(rng, extent, jnp.float32)
    if cuts:
        array = array * level_of(rng, extent, cuts, -0.22, 0.18)
    return jnp.clip(array, -limit, limit).astype(kind)


def setup_inputs(seed: int = 0) -> dict:
    splits = jax.random.split(jax.random.key(seed), 15)
    clean_latents = noise(splits[0], (NF, NR, W, D), 1.0, 6.0, ((0, 8), (1, 32)))
    gaussian_noise = noise(splits[1], (NF, NR, W, D), 1.0, 6.0, ((0, 8), (1, 32)))
    text_states = noise(splits[2], (TXT, D), 1.0, 6.0)
    queries = draw_queries(jax.random.fold_in(splits[14], 71), 0)
    key_states = draw_key_states(jax.random.fold_in(splits[14], 71), 0)
    cotangent = noise(splits[5], (NF, NR, W, HD), 40.0, 240.0, ((0, 8), (1, 32)))
    text_keys = noise(splits[6], (TXT, HD), 1.0, 6.0)
    window_radii = with_ends(jax.random.randint(splits[7], (HEADS, 3), 0, 2), jax.random.fold_in(splits[7], 1), 0, 1).astype(jnp.int32)
    timestep = jax.random.randint(splits[8], (1,), 200, 800).astype(jnp.int32)
    sketch_seed = jax.random.randint(splits[9], (1,), 0, 65536).astype(jnp.int32)
    down_image = noise(splits[10], (D, RANK), D ** -0.5, 0.109375)
    up_image = noise(splits[11], (RANK, HD), RANK ** -0.5, 1.5)
    down_text = noise(splits[12], (D, RANK), D ** -0.5, 0.109375)
    up_text = noise(splits[13], (RANK, HD), RANK ** -0.5, 1.5)
    return {"clean_latents": clean_latents, "gaussian_noise": gaussian_noise, "text_states": text_states, "queries": queries, "key_states": key_states, "cotangent": cotangent, "text_keys": text_keys, "window_radii": window_radii, "timestep": timestep, "sketch_seed": sketch_seed, "down_image": down_image, "up_image": up_image, "down_text": down_text, "up_text": up_text}


def tile_rows(block, width):
    frame_count, row_count, col_count = block.shape[0], block.shape[1], block.shape[2]
    rest = block.shape[3:]
    col_tiles = col_count // width
    shaped = block.reshape((frame_count, row_count, col_tiles, width) + rest)
    order = (2, 0, 1, 3) + tuple(range(4, 4 + len(rest)))
    return jnp.transpose(shaped, order).reshape((col_tiles, frame_count * row_count * width) + rest)


def region_rows(padded, width):
    col_count = padded.shape[2] - 2 * width
    views = [tile_rows(padded[:, :, shift_col * width:shift_col * width + col_count], width) for shift_col in range(3)]
    return jnp.concatenate(views, axis=1)


def window_mask(radius, frame_tile, row_tile, frame_tiles, row_tiles, col_tiles, frame_count, row_count, width):
    region = 27 * frame_count * row_count * width
    position = jnp.arange(region, dtype=jnp.int32)
    col_step = position // (9 * frame_count * row_count * width) - 1
    frame_step = (position // (3 * row_count * width)) % (3 * frame_count) // frame_count - 1
    row_step = (position // width) % (3 * row_count) // row_count - 1
    inside = (jnp.abs(frame_step) <= radius[0]) & (jnp.abs(row_step) <= radius[1]) & (jnp.abs(col_step) <= radius[2])
    inside = inside & (frame_tile + frame_step >= 0) & (frame_tile + frame_step < frame_tiles)
    inside = inside & (row_tile + row_step >= 0) & (row_tile + row_step < row_tiles)
    col_index = jnp.arange(col_tiles, dtype=jnp.int32)[:, None]
    return inside[None, :] & (col_index + col_step[None, :] >= 0) & (col_index + col_step[None, :] < col_tiles)


def forward_head(query_head, key_region, text_head, cot_head, allowed, score_scale):
    image_scores = jnp.einsum('cqd,cld->cql', query_head.astype(jnp.float32), key_region.astype(jnp.float32)) * score_scale
    image_scores = jnp.where(allowed[:, None, :], image_scores, -jnp.inf)
    text_scores = jnp.einsum('cqd,td->cqt', query_head.astype(jnp.float32), text_head.astype(jnp.float32)) * score_scale
    row_max = jnp.maximum(jnp.max(image_scores, axis=-1), jnp.max(text_scores, axis=-1))
    total = jnp.sum(jnp.exp(image_scores - row_max[..., None]), axis=-1) + jnp.sum(jnp.exp(text_scores - row_max[..., None]), axis=-1)
    log_total = row_max + jnp.log(total)
    text_probs = jnp.exp(text_scores - log_total[..., None]).astype(jnp.bfloat16)
    text_part = jnp.einsum('cqt,cqd->td', text_probs.astype(jnp.float32), cot_head.astype(jnp.float32))
    return log_total, text_part


def backward_head(query_region, cot_region, key_head, log_region, allowed, score_scale):
    scores = jnp.einsum('cld,cqd->clq', query_region.astype(jnp.float32), key_head.astype(jnp.float32)) * score_scale
    probs = jnp.where(allowed[:, :, None], jnp.exp(scores - log_region[..., None]), 0.0).astype(jnp.bfloat16)
    return jnp.einsum('clq,cld->cqd', probs.astype(jnp.float32), cot_region.astype(jnp.float32))


def sketch_signs(seed_value, rows, width):
    row_part = jnp.arange(rows, dtype=jnp.int32)[:, None] * width
    position = row_part + jnp.arange(width, dtype=jnp.int32)[None, :]
    mixed_bits = position * 1103515245 + seed_value * 12345 + 1013904223
    mixed_bits = mixed_bits ^ (mixed_bits >> 16)
    mixed_bits = mixed_bits * 73244475
    mixed_bits = mixed_bits ^ (mixed_bits >> 16)
    return (1 - 2 * ((mixed_bits >> 7) & 1)).astype(jnp.float32)


def count_sketch(pieces, seed_value, width, sketch_scale):
    flat = jnp.concatenate([piece.reshape(-1) for piece in pieces]).reshape(-1, width)
    signed = flat * sketch_signs(seed_value, flat.shape[0], width)
    return jnp.sum(signed, axis=0) * sketch_scale


def mat_product(left, right):
    return jnp.dot(left.astype(jnp.float32), right.astype(jnp.float32), precision=lax.Precision.HIGHEST)


def reference(clean_latents, gaussian_noise, text_states, queries, key_states, cotangent, text_keys, window_radii, timestep, sketch_seed, down_image, up_image, down_text, up_text):
    col_tiles = W // TW
    score_scale = HDIM ** -0.5
    pad_spec = ((FT, FT), (HR, HR), (TW, TW), (0, 0))
    key_pad = jnp.pad(key_states, pad_spec)
    zero_start = jnp.zeros((), jnp.int32)
    block_ids = jnp.arange(N_TM * N_HEIGHT, dtype=jnp.int32)
    head_ids = jnp.arange(HEADS, dtype=jnp.int32)

    def block_start(block_index):
        frame_tile = (block_index // N_HEIGHT).astype(jnp.int32)
        row_tile = (block_index % N_HEIGHT).astype(jnp.int32)
        return frame_tile, row_tile, ((frame_tile * FT).astype(jnp.int32), (row_tile * HR).astype(jnp.int32), zero_start, zero_start)

    def split_heads(block, axis):
        moved = jnp.moveaxis(block, axis, -1)
        shaped = moved.reshape(moved.shape[:-1] + (HEADS, HDIM))
        return jnp.moveaxis(shaped, -2, 0)

    def forward_block(carry, block_index):
        frame_tile, row_tile, start = block_start(block_index)
        own_q = split_heads(tile_rows(lax.dynamic_slice(queries, start, (FT, HR, W, HD)), TW), 2)
        own_c = split_heads(tile_rows(lax.dynamic_slice(cotangent, start, (FT, HR, W, HD)), TW), 2)
        near_k = split_heads(region_rows(lax.dynamic_slice(key_pad, start, (3 * FT, 3 * HR, W + 2 * TW, HD)), TW), 2)
        text_h = split_heads(text_keys, 1)

        def per_head(head_index, query_head, key_region, text_head, cot_head):
            allowed = window_mask(window_radii[head_index], frame_tile, row_tile, N_TM, N_HEIGHT, col_tiles, FT, HR, TW)
            return forward_head(query_head, key_region, text_head, cot_head, allowed, score_scale)

        log_total, text_part = jax.vmap(per_head)(head_ids, own_q, near_k, text_h, own_c)
        text_part = jnp.transpose(text_part, (1, 0, 2)).reshape(TXT, HD)
        return carry + text_part, log_total

    text_value, log_blocks = lax.scan(forward_block, jnp.zeros((TXT, HD), jnp.float32), block_ids)
    log_tokens = log_blocks.reshape(N_TM, N_HEIGHT, HEADS, col_tiles, FT, HR, TW)
    log_tokens = jnp.transpose(log_tokens, (0, 4, 1, 5, 3, 6, 2)).reshape(NF, NR, W, HEADS)
    query_pad = jnp.pad(queries, pad_spec)
    cot_pad = jnp.pad(cotangent, pad_spec)
    log_pad = jnp.pad(log_tokens, pad_spec)

    def backward_block(block_index):
        frame_tile, row_tile, start = block_start(block_index)
        own_k = split_heads(tile_rows(lax.dynamic_slice(key_states, start, (FT, HR, W, HD)), TW), 2)
        near_q = split_heads(region_rows(lax.dynamic_slice(query_pad, start, (3 * FT, 3 * HR, W + 2 * TW, HD)), TW), 2)
        near_c = split_heads(region_rows(lax.dynamic_slice(cot_pad, start, (3 * FT, 3 * HR, W + 2 * TW, HD)), TW), 2)
        log_region = jnp.moveaxis(region_rows(lax.dynamic_slice(log_pad, start, (3 * FT, 3 * HR, W + 2 * TW, HEADS)), TW), 2, 0)

        def per_head(head_index, query_region, cot_region, key_head, head_log):
            allowed = window_mask(window_radii[head_index], frame_tile, row_tile, N_TM, N_HEIGHT, col_tiles, FT, HR, TW)
            return backward_head(query_region, cot_region, key_head, head_log, allowed, score_scale)

        return jax.vmap(per_head)(head_ids, near_q, near_c, own_k, log_region)

    grads = lax.map(backward_block, block_ids)
    grads = grads.reshape(N_TM, N_HEIGHT, HEADS, col_tiles, FT, HR, TW, HDIM)
    value_f32 = jnp.transpose(grads, (0, 4, 1, 5, 3, 6, 2, 7)).reshape(NF, NR, W, HD)
    value_grad = value_f32.astype(jnp.bfloat16)

    noise_level = timestep[0].astype(jnp.float32) / 1000.0
    mixed = ((1.0 - noise_level) * clean_latents.astype(jnp.float32) + noise_level * gaussian_noise.astype(jnp.float32)).astype(jnp.bfloat16)
    mixed = mixed.reshape(TOKENS, D)
    flat_value = value_grad.reshape(TOKENS, HD)
    hidden = mat_product(mixed, down_image).astype(jnp.bfloat16)
    grad_up = mat_product(hidden.T, flat_value)
    backward_low = mat_product(flat_value, up_image.T).astype(jnp.bfloat16)
    grad_down = mat_product(mixed.T, backward_low)
    text_hidden = mat_product(text_states, down_text)
    text_up_grad = mat_product(text_hidden.T, text_value)
    text_back = mat_product(text_value, up_text.T)
    text_down_grad = mat_product(text_states.T, text_back)
    sketch_scale = (TOKENS * (PARAMS // SKETCH)) ** -0.5
    grad_sketch = count_sketch((grad_down, grad_up, text_down_grad, text_up_grad), sketch_seed[0], SKETCH, sketch_scale)
    return value_grad, grad_sketch
```

```python
import functools

import jax
import jax.numpy as jnp
from jax import lax
from jax.experimental import pallas as pl
from jax.experimental.pallas import tpu as pltpu
from jax.sharding import PartitionSpec as P

MESH = pl.DeviceIdType.MESH
TW = 8
LANES = 128
SKETCH = 16384
NEG = -1e30
LOG2E = 1.4426950408889634
OWN, PART, FAR = 0, 1, 2
AHEAD = 3


def dot(a, b, ca, cb):
    return lax.dot_general(a, b, (((ca,), (cb,)), ((), ())), preferred_element_type=jnp.float32)


def remote(src, dst, ssem, rsem, device):
    return pltpu.make_async_remote_copy(
        src_ref=src, dst_ref=dst, send_sem=ssem, recv_sem=rsem, device_id=device, device_id_type=MESH
    )


def attention_kernel(
    n_a, n_b, heads, frames, rows,
    meta, closed, q_ref, k_ref, c_ref, tk_ref, vg_ref, tv_ref,
    by_head, kr, gp, ga, gf, gy, gz, vgs, tvs, s_ref, p_ref,
    kz_s, kz_r, ky_s, ky_r, kf_s, kf_r, gf_s, gf_r, gy_s, gy_r, gz_s, gz_r,
):
    n_rows = n_a + n_b
    tile = k_ref.shape[0]
    f = lax.axis_index("tm")
    h = lax.axis_index("height")
    even = lax.rem(h, 2) == 0
    partner = (f, h + 1 - 2 * lax.rem(h, 2))
    step = 2 - 4 * lax.rem(h, 2)
    has_to = (h + step >= 0) & (h + step < rows)
    has_from = (h - step >= 0) & (h - step < rows)
    far_to = (f, jnp.where(has_to, h + step, h))
    far_from = (f, jnp.where(has_from, h - step, h))
    has_low = f > 0
    has_high = f < frames - 1
    low = (jnp.maximum(f - 1, 0), h)
    high = (jnp.minimum(f + 1, frames - 1), h)
    sides = ((low, has_low), (high, has_high))

    barrier = pltpu.get_barrier_semaphore()
    peers = [(low, has_low), (high, has_high)]
    if n_rows:
        peers += [(far_to, has_to), (far_from, has_from)]
        pl.semaphore_signal(barrier, inc=1, device_id=partner, device_id_type=MESH)
    for peer, exists in peers:
        @pl.when(exists)
        def _(peer=peer):
            pl.semaphore_signal(barrier, inc=1, device_id=peer, device_id_type=MESH)

    for n, ref in enumerate((k_ref, q_ref, c_ref, tk_ref)):
        for j in range(heads):
            by_head[n, j] = ref[:, j * LANES:(j + 1) * LANES]

    @pl.loop(0, heads)
    def _(s):
        kr[s, 0] = by_head[0, meta[0, s]]

    for side, exists in enumerate((has_low, has_high)):
        @pl.when(jnp.logical_not(exists))
        def _(side=side):
            @pl.loop(0, heads)
            def _(s):
                for row in range(3):
                    kr[s, 3 * (1 + side) + row] = jnp.zeros((tile, LANES), jnp.bfloat16)

    @pl.when(jnp.logical_not(has_from))
    def _():
        @pl.loop(0, heads)
        def _(s):
            for t in (FAR, 3 + FAR, 6 + FAR):
                kr[s, t] = jnp.zeros((tile, LANES), jnp.bfloat16)

    arrivals = 1 if n_rows else 0
    for peer, exists in peers:
        arrivals = arrivals + jnp.where(exists, 1, 0)
    pl.semaphore_wait(barrier, arrivals)

    def k_cross(s):
        return remote(kr.at[s, OWN], kr.at[s, PART], kz_s.at[s], kz_r.at[s], partner)

    def k_far(s):
        return remote(kr.at[s, PART], kr.at[s, FAR], ky_s.at[s], ky_r.at[s], far_to)

    def k_frame(s, side, row):
        return remote(
            kr.at[s, row], kr.at[s, 3 * (2 - side) + row],
            kf_s.at[s, side, row], kf_r.at[s, 1 - side, row], sides[side][0],
        )

    def k_frame_in(s, side, row):
        return remote(
            kr.at[s, row], kr.at[s, 3 * (1 + side) + row],
            kf_s.at[s, side, row], kf_r.at[s, side, row], sides[side][0],
        )

    def g_frame(s, side, row):
        return remote(
            gp.at[s, 3 * (1 + side) + row], gf.at[s, 1 - side, row],
            gf_s.at[s, side, row], gf_r.at[s, 1 - side, row], sides[side][0],
        )

    def g_frame_in(s, side, row):
        return remote(
            gp.at[s, 3 * (1 + side) + row], gf.at[s, side, row],
            gf_s.at[s, side, row], gf_r.at[s, side, row], sides[side][0],
        )

    def g_far(s):
        return remote(gp.at[s, FAR], gy.at[s], gy_s.at[s], gy_r.at[s], far_from)

    def g_cross(s):
        return remote(gp.at[s, PART], gz.at[s], gz_s.at[s], gz_r.at[s], partner)

    def each_side(fn, extra=None):
        for side in range(2):
            cond = sides[side][1] if extra is None else sides[side][1] & extra

            @pl.when(cond)
            def _(side=side):
                fn(side)

    def row_exists(row):
        return has_from if row == FAR else None

    lane = lax.broadcasted_iota(jnp.int32, (2, 8, tile), 2)
    group = lax.broadcasted_iota(jnp.int32, (2, 8, tile), 0)
    cross_col = jnp.where(lax.rem(lane // TW, 2) != group, 1.0, 0.0)
    to_log2 = jnp.float32(LANES**-0.5 * LOG2E)

    def attend(s, tiles):
        head = meta[0, s]
        q = by_head[1, head]
        bias = cross_col * closed[2, s]
        top = None
        for n, t in enumerate([None] + tiles):
            keys = by_head[3, head] if t is None else kr[s, t]
            sc = dot(keys, q, 1, 1)
            if t is not None:
                limit = bias
                if t // 3:
                    limit = limit + closed[0, s] + jnp.where(sides[t // 3 - 1][1], 0.0, NEG)
                if t % 3:
                    limit = limit + closed[1, s]
                if t % 3 == FAR:
                    limit = limit + jnp.where(has_from, 0.0, NEG)
                sc = (sc.reshape(tile // 16, 2, 8, tile) + limit).reshape(tile, tile)
            s_ref[n * tile:(n + 1) * tile, :] = sc
            m = jnp.max(sc.reshape(tile // 8, 8, tile), axis=0)
            top = m if top is None else jnp.maximum(top, m)
        top = jnp.max(top, axis=0, keepdims=True)
        total = jnp.zeros((8, tile), jnp.float32)
        for n in range(len(tiles) + 1):
            e = jnp.exp2((s_ref[n * tile:(n + 1) * tile, :] - top) * to_log2)
            total = total + jnp.sum(e.reshape(tile // 8, 8, tile), axis=0)
            p_ref[n * tile:(n + 1) * tile, :] = e.astype(jnp.bfloat16)
        total = jnp.sum(total, axis=0, keepdims=True)
        inverse = jnp.transpose(jnp.broadcast_to(1.0 / total, (8, tile)))[:, :1]
        cot = (by_head[2, head].astype(jnp.float32) * inverse).astype(jnp.bfloat16)
        for n, t in enumerate([None] + tiles):
            g = dot(p_ref[n * tile:(n + 1) * tile, :], cot, 1, 0)
            if t is None:
                tvs[s] = g
            elif t < 3:
                ga[s, t] = g
            else:
                gp[s, t] = g.astype(jnp.bfloat16)

    def in_range(i, lo, hi, fn):
        if hi > lo:
            @pl.when((i >= lo) & (i < hi))
            def _():
                fn(i)

    def start_frames(s, row):
        each_side(lambda side: k_frame(s, side, row).start(), row_exists(row))

    def pass_partner(s):
        k_cross(s).wait_recv()

        @pl.when(has_to)
        def _():
            k_far(s).start()
        in_range(s, 0, n_a, lambda s: start_frames(s, PART))

    def pass_far(s):
        @pl.when(has_from)
        def _():
            k_far(s).wait_recv()
        in_range(s, 0, n_a, lambda s: start_frames(s, FAR))

    def frames_in(s, row_list):
        for row in row_list:
            each_side(lambda side: k_frame_in(s, side, row).wait_recv(), row_exists(row))

    def frames_out(s, row_list):
        for row in row_list:
            each_side(lambda side: g_frame(s, side, row).start(), row_exists(row))

    def compute_a(s):
        frames_in(s, range(3))
        attend(s, list(range(9)))
        frames_out(s, (FAR, PART, OWN))

    def compute_b(s):
        attend(s, [0, 1, 2])

    def compute_c(s):
        frames_in(s, [OWN])
        attend(s, [0, 3, 6])
        frames_out(s, [OWN])

    def add_frames(s, row):
        def add(side):
            g_frame_in(s, side, row).wait_recv()
            ga[s, row] = ga[s, row] + gf[s, side, row].astype(jnp.float32)
        each_side(add, row_exists(row))

    def reduce_far(s):
        in_range(s, 0, n_a, lambda s: add_frames(s, FAR))

        @pl.when(has_from)
        def _():
            gp[s, FAR] = ga[s, FAR].astype(jnp.bfloat16)
            g_far(s).start()

    def reduce_partner(s):
        in_range(s, 0, n_a, lambda s: add_frames(s, PART))

        @pl.when(has_to)
        def _():
            g_far(s).wait_recv()
            ga[s, PART] = ga[s, PART] + gy[s].astype(jnp.float32)
        gp[s, PART] = ga[s, PART].astype(jnp.bfloat16)
        g_cross(s).start()

    def finish(s):
        in_range(s, 0, n_a, lambda s: add_frames(s, OWN))
        in_range(s, n_rows, heads, lambda s: add_frames(s, OWN))
        if n_rows:
            @pl.when(s < n_rows)
            def _():
                g_cross(s).wait_recv()
                ga[s, OWN] = ga[s, OWN] + gz[s].astype(jnp.float32)
        vgs[s] = ga[s, OWN].astype(jnp.bfloat16)

    for s in range(min(AHEAD, n_rows)):
        k_cross(s).start()

    @pl.loop(0, heads)
    def _(s):
        in_range(s, 0, n_a, lambda s: start_frames(s, OWN))
        in_range(s, n_rows, heads, lambda s: start_frames(s, OWN))

    @pl.loop(0, heads + 6)
    def _(i):
        in_range(i + AHEAD, 0, n_rows, lambda s: k_cross(s).start())
        in_range(i, 0, n_rows, pass_partner)
        in_range(i - 1, 0, n_rows, pass_far)
        in_range(i - 2, 0, n_a, compute_a)
        in_range(i - 2, n_a, n_rows, compute_b)
        in_range(i - 2, n_rows, heads, compute_c)
        in_range(i - 3, 0, n_rows, reduce_far)
        in_range(i - 4, 0, n_rows, reduce_partner)
        in_range(i - 6, 0, heads, finish)

    for j in range(heads):
        slot = meta[1, j]
        vg_ref[:, j * LANES:(j + 1) * LANES] = vgs[slot]
        tv_ref[:, j * LANES:(j + 1) * LANES] = tvs[slot]

    @pl.loop(0, heads)
    def _(s):
        def sent_rows(s):
            k_cross(s).wait_send()
            g_cross(s).wait_send()

            @pl.when(has_to)
            def _():
                k_far(s).wait_send()

            @pl.when(has_from)
            def _():
                g_far(s).wait_send()

        def sent_frames(s, row_list):
            for row in row_list:
                each_side(lambda side: k_frame(s, side, row).wait_send(), row_exists(row))
                each_side(lambda side: g_frame(s, side, row).wait_send(), row_exists(row))
        in_range(s, 0, n_rows, sent_rows)
        in_range(s, 0, n_a, lambda s: sent_frames(s, range(3)))
        in_range(s, n_rows, heads, lambda s: sent_frames(s, [OWN]))


def attention(n_a, n_b, cid, frames, rows, meta, closed, q, k, c, tk):
    tile, width = k.shape
    heads = width // LANES
    vmem = pl.BlockSpec(memory_space=pltpu.VMEM)
    sem = pltpu.SemaphoreType.DMA
    bf, f32 = jnp.bfloat16, jnp.float32
    box = (tile, LANES)
    return pl.pallas_call(
        functools.partial(attention_kernel, n_a, n_b, heads, frames, rows),
        out_shape=(jax.ShapeDtypeStruct((tile, width), bf), jax.ShapeDtypeStruct((tile, width), f32)),
        in_specs=[pl.BlockSpec(memory_space=pltpu.SMEM)] * 2 + [vmem] * 4,
        out_specs=(vmem, vmem),
        scratch_shapes=[
            pltpu.VMEM((4, heads) + box, bf),
            pltpu.VMEM((heads, 9) + box, bf),
            pltpu.VMEM((heads, 9) + box, bf),
            pltpu.VMEM((heads, 3) + box, f32),
            pltpu.VMEM((heads, 2, 3) + box, bf),
            pltpu.VMEM((heads,) + box, bf),
            pltpu.VMEM((heads,) + box, bf),
            pltpu.VMEM((heads,) + box, bf),
            pltpu.VMEM((heads,) + box, f32),
            pltpu.VMEM((10 * tile, tile), f32),
            pltpu.VMEM((10 * tile, tile), bf),
            sem((heads,)), sem((heads,)), sem((heads,)), sem((heads,)),
            sem((heads, 2, 3)), sem((heads, 2, 3)), sem((heads, 2, 3)), sem((heads, 2, 3)),
            sem((heads,)), sem((heads,)), sem((heads,)), sem((heads,)),
        ],
        compiler_params=pltpu.CompilerParams(
            collective_id=cid, has_side_effects=True, vmem_limit_bytes=56 << 20
        ),
    )(meta, closed, q, k, c, tk)


def split2(x):
    hi = x.astype(jnp.bfloat16)
    return hi, (x - hi.astype(jnp.float32)).astype(jnp.bfloat16)


def sketch_kernel(
    token_total,
    time_ref, seed_ref, vg_ref, tv_ref, clean_ref, noise_ref, text_ref,
    di_ref, ui_ref, dt_ref, ut_ref, out_ref,
    flat, part, box1, box2, s_sem, r_sem,
):
    f = lax.axis_index("tm")
    h = lax.axis_index("height")
    g = 2 * f + lax.rem(h, 2)
    w = h // 2
    count = 16

    def in_ring(i):
        return (i // 2, 2 * w + lax.rem(i, 2))

    def in_plane(i):
        return (f, 2 * i + lax.rem(h, 2))

    barrier = pltpu.get_barrier_semaphore()

    @pl.loop(1, count)
    def _(k):
        pl.semaphore_signal(barrier, inc=1, device_id=in_ring(lax.rem(g + k, count)), device_id_type=MESH)
        pl.semaphore_signal(barrier, inc=1, device_id=in_plane(lax.rem(w + k, count)), device_id_type=MESH)

    width = vg_ref.shape[1]
    depth = clean_ref.shape[1]
    rank = ui_ref.shape[0]
    copies = LANES // rank
    level = jnp.full((1, depth), time_ref[0], jnp.int32).astype(jnp.float32) / 1000.0
    mixed = (
        (1.0 - level) * clean_ref[...].astype(jnp.float32) + level * noise_ref[...].astype(jnp.float32)
    ).astype(jnp.bfloat16)
    vg = vg_ref[...]
    hidden = dot(mixed, di_ref[...], 1, 0).astype(jnp.bfloat16)
    up_image = dot(hidden, vg, 0, 0)
    ui_wide = jnp.concatenate([ui_ref[...]] * copies, axis=0)
    ut_wide = jnp.concatenate([ut_ref[...]] * copies, axis=0)
    back = dot(vg, ui_wide, 1, 1).astype(jnp.bfloat16)
    lane8 = lax.broadcasted_iota(jnp.int32, (1, copies, LANES), 2)
    row8 = lax.broadcasted_iota(jnp.int32, (1, copies, LANES), 1)
    pick = lane8 // rank == row8

    def place_down(base, wide):
        kept = jnp.where(pick, wide.reshape(-1, copies, LANES), 0.0)
        flat[base:base + depth // copies, :] = jnp.sum(kept, axis=1)

    def place_up(base, grad):
        per = width // LANES
        for r in range(rank):
            for m in range(per):
                row = base + r * per + m
                flat[row:row + 1, :] = grad[r:r + 1, m * LANES:(m + 1) * LANES]

    place_down(0, dot(mixed, back, 0, 0))
    place_up(384, up_image)
    text = text_ref[...]
    tv_hi, tv_lo = split2(tv_ref[...])
    th_hi, th_lo = split2(dot(text, dt_ref[...], 1, 0))
    place_up(960, dot(th_hi, tv_hi, 0, 0) + (dot(th_hi, tv_lo, 0, 0) + dot(th_lo, tv_hi, 0, 0)))
    tb_hi, tb_lo = split2(dot(tv_hi, ut_wide, 1, 1) + dot(tv_lo, ut_wide, 1, 1))
    place_down(576, dot(text, tb_hi, 0, 0) + dot(text, tb_lo, 0, 0))

    total_rows = flat.shape[0]
    pos = lax.broadcasted_iota(jnp.int32, (total_rows, LANES), 0) * LANES
    pos = pos + lax.broadcasted_iota(jnp.int32, (total_rows, LANES), 1)
    bits = pos * 1103515245 + seed_ref[0] * 12345 + 1013904223
    bits = bits ^ (bits >> 16)
    bits = bits * 73244475
    bits = bits ^ (bits >> 16)
    signs = (1 - 2 * ((bits >> 7) & 1)).astype(jnp.float32)
    rows = SKETCH // LANES
    pieces = total_rows // rows
    scale = (token_total * pieces) ** -0.5
    signed = flat[...] * signs
    acc = signed[0:rows]
    for m in range(1, pieces):
        acc = acc + signed[m * rows:(m + 1) * rows]
    chunk = rows // count
    part[...] = (acc * scale).reshape(count, chunk, LANES)

    pl.semaphore_wait(barrier, 2 * (count - 1))

    def send1(k):
        i = lax.rem(g + k, count)
        return remote(part.at[i], box1.at[g], s_sem.at[0, k], r_sem.at[0, g], in_ring(i))

    def send2(k):
        i = lax.rem(w + k, count)
        return remote(box2.at[w], box2.at[w], s_sem.at[1, k], r_sem.at[1, w], in_plane(i))

    def send3(k):
        i = lax.rem(g + k, count)
        return remote(out_ref.at[g], out_ref.at[g], s_sem.at[2, k], r_sem.at[2, g], in_ring(i))

    def recv(phase, dst, i):
        return remote(dst.at[i], dst.at[i], s_sem.at[phase, 0], r_sem.at[phase, i], in_ring(lax.rem(g + 1, count)))

    def phase(n, me, dst, send):
        @pl.loop(1, count)
        def _(k):
            send(k).start()

        @pl.loop(1, count)
        def _(k):
            recv(n, dst, lax.rem(me + k, count)).wait_recv()

    box1[g] = part[g]
    phase(0, g, box1, send1)
    box2[w] = jnp.sum(box1[...], axis=0)
    phase(1, w, box2, send2)
    out_ref[g] = jnp.sum(box2[...], axis=0)
    phase(2, g, out_ref, send3)

    @pl.loop(1, count)
    def _(k):
        send1(k).wait_send()
        send2(k).wait_send()
        send3(k).wait_send()


def sketch(cid, token_total, *args):
    vmem = pl.BlockSpec(memory_space=pltpu.VMEM)
    smem = pl.BlockSpec(memory_space=pltpu.SMEM)
    rows = SKETCH // LANES
    f32 = jnp.float32
    return pl.pallas_call(
        functools.partial(sketch_kernel, token_total),
        out_shape=jax.ShapeDtypeStruct((16, rows // 16, LANES), f32),
        in_specs=[smem, smem] + [vmem] * 9,
        out_specs=vmem,
        scratch_shapes=[
            pltpu.VMEM((9 * rows, LANES), f32),
            pltpu.VMEM((16, rows // 16, LANES), f32),
            pltpu.VMEM((16, rows // 16, LANES), f32),
            pltpu.VMEM((16, rows // 16, LANES), f32),
            pltpu.SemaphoreType.DMA((3, 16)),
            pltpu.SemaphoreType.DMA((3, 16)),
        ],
        compiler_params=pltpu.CompilerParams(
            collective_id=cid, has_side_effects=True, vmem_limit_bytes=56 << 20
        ),
    )(*args)


VARIANTS = ((12, 0),)


def assign(radii, variants, heads):
    far_f = radii[:, 0] > 0
    far_r = radii[:, 1] > 0
    kind = jnp.where(far_r, jnp.where(far_f, 0, 1), jnp.where(far_f, 2, 3))
    n = [jnp.sum(kind == t) for t in range(4)]
    choice = jnp.int32(len(variants) - 1)
    a, b = jnp.int32(variants[-1][0]), jnp.int32(variants[-1][1])
    for i in reversed(range(len(variants) - 1)):
        va, vb = variants[i]
        vc = heads - va - vb
        fits = (n[0] <= va) & (n[0] + n[1] <= va + vb) & (n[0] + n[2] <= va + vc)
        choice = jnp.where(fits, i, choice)
        a, b = jnp.where(fits, va, a), jnp.where(fits, vb, b)
    c = heads - a - b
    before = jnp.tril(jnp.ones((heads, heads), jnp.int32), -1)
    rank = jnp.sum(before * (kind[:, None] == kind[None, :]), axis=1)
    over_b = jnp.maximum(n[1] - b, 0)
    over_c = jnp.maximum(n[2] - c, 0)
    spare_a = a - n[0] - over_b - over_c
    spare_b = b - (n[1] - over_b)
    slot_a = rank
    slot_b = jnp.where(rank < over_b, n[0] + rank, a + rank - over_b)
    slot_c = jnp.where(rank < over_c, n[0] + over_b + rank, heads - (n[2] - over_c) + rank - over_c)
    slot_d = jnp.where(
        rank < spare_a,
        n[0] + over_b + over_c + rank,
        jnp.where(rank < spare_a + spare_b, a + (n[1] - over_b) + rank - spare_a, a + b + rank - spare_a - spare_b),
    )
    slot = jnp.where(kind == 0, slot_a, jnp.where(kind == 1, slot_b, jnp.where(kind == 2, slot_c, slot_d)))
    hit = (slot[None, :] == jnp.arange(heads)[:, None]).astype(jnp.int32)
    table = jnp.concatenate([jnp.arange(heads, dtype=jnp.int32)[:, None], radii.astype(jnp.int32)], axis=1)
    by_slot = jnp.sum(hit[:, :, None] * table[None], axis=1)
    meta = jnp.concatenate([by_slot[:, :1].T, slot[None].astype(jnp.int32)], axis=0)
    closed = jnp.where(by_slot[:, 1:].T > 0, 0.0, NEG)
    return choice, meta, closed


def per_device(
    clean_latents, gaussian_noise, text_states, queries, key_states, cotangent, text_keys,
    window_radii, timestep, sketch_seed, down_image, up_image, down_text, up_text,
):
    width = queries.shape[-1]
    depth = clean_latents.shape[-1]
    heads = window_radii.shape[0]
    frames, rows = lax.axis_size("tm"), lax.axis_size("height")
    choice, meta, closed = assign(window_radii, VARIANTS, heads)
    branches = [
        functools.partial(attention, a, b, i + 1, frames, rows) for i, (a, b) in enumerate(VARIANTS)
    ]
    operands = (
        meta,
        closed,
        queries.reshape(-1, width),
        key_states.reshape(-1, width),
        cotangent.reshape(-1, width),
        text_keys,
    )
    if len(branches) == 1:
        vg, tv = branches[0](*operands)
    else:
        vg, tv = lax.switch(choice, branches, *operands)
    tokens = vg.shape[0] * frames * rows
    sk = sketch(
        0, tokens, timestep, sketch_seed, vg, tv,
        clean_latents.reshape(-1, depth), gaussian_noise.reshape(-1, depth), text_states,
        down_image, up_image, down_text, up_text,
    )
    return vg.reshape(queries.shape), sk.reshape(-1)


def solution(mesh):
    block = P("tm", "height", None, None)
    return jax.shard_map(
        per_device,
        mesh=mesh,
        in_specs=(block, block, P(), block, block, block) + (P(),) * 8,
        out_specs=(block, P()),
        check_vma=False,
    )
```

```python
import functools

import jax
import jax.numpy as jnp
from jax import lax
from jax.experimental import pallas as pl
from jax.experimental.pallas import tpu as pltpu
from jax.sharding import PartitionSpec as P

MESH = pl.DeviceIdType.MESH
TW = 8
LANES = 128
SKETCH = 16384
NEG = -1e30
LOG2E = 1.4426950408889634
OWN, PART, FAR = 0, 1, 2
AHEAD = 3


def dot(a, b, ca, cb):
    return lax.dot_general(a, b, (((ca,), (cb,)), ((), ())), preferred_element_type=jnp.float32)


def remote(src, dst, ssem, rsem, device):
    return pltpu.make_async_remote_copy(
        src_ref=src, dst_ref=dst, send_sem=ssem, recv_sem=rsem, device_id=device, device_id_type=MESH
    )


def attention_kernel(
    n_a, n_b, heads, frames, rows,
    meta, closed, q_ref, k_ref, c_ref, tk_ref, vg_ref, tv_ref,
    by_head, kr, gp, ga, gf, gy, gz, vgs, tvs, s_ref, p_ref,
    kz_s, kz_r, ky_s, ky_r, kf_s, kf_r, gf_s, gf_r, gy_s, gy_r, gz_s, gz_r,
):
    n_rows = n_a + n_b
    tile = k_ref.shape[0]
    f = lax.axis_index("tm")
    h = lax.axis_index("height")
    even = lax.rem(h, 2) == 0
    partner = (f, h + 1 - 2 * lax.rem(h, 2))
    step = 2 - 4 * lax.rem(h, 2)
    has_to = (h + step >= 0) & (h + step < rows)
    has_from = (h - step >= 0) & (h - step < rows)
    far_to = (f, jnp.where(has_to, h + step, h))
    far_from = (f, jnp.where(has_from, h - step, h))
    has_low = f > 0
    has_high = f < frames - 1
    low = (jnp.maximum(f - 1, 0), h)
    high = (jnp.minimum(f + 1, frames - 1), h)
    sides = ((low, has_low), (high, has_high))

    barrier = pltpu.get_barrier_semaphore()
    peers = [(low, has_low), (high, has_high)]
    if n_rows:
        peers += [(far_to, has_to), (far_from, has_from)]
        pl.semaphore_signal(barrier, inc=1, device_id=partner, device_id_type=MESH)
    for peer, exists in peers:
        @pl.when(exists)
        def _(peer=peer):
            pl.semaphore_signal(barrier, inc=1, device_id=peer, device_id_type=MESH)

    for n, ref in enumerate((k_ref, q_ref, c_ref, tk_ref)):
        for j in range(heads):
            by_head[n, j] = ref[:, j * LANES:(j + 1) * LANES]

    @pl.loop(0, heads)
    def _(s):
        kr[s, 0] = by_head[0, meta[0, s]]

    for side, exists in enumerate((has_low, has_high)):
        @pl.when(jnp.logical_not(exists))
        def _(side=side):
            @pl.loop(0, heads)
            def _(s):
                for row in range(3):
                    kr[s, 3 * (1 + side) + row] = jnp.zeros((tile, LANES), jnp.bfloat16)

    @pl.when(jnp.logical_not(has_from))
    def _():
        @pl.loop(0, heads)
        def _(s):
            for t in (FAR, 3 + FAR, 6 + FAR):
                kr[s, t] = jnp.zeros((tile, LANES), jnp.bfloat16)

    arrivals = 1 if n_rows else 0
    for peer, exists in peers:
        arrivals = arrivals + jnp.where(exists, 1, 0)
    pl.semaphore_wait(barrier, arrivals)

    def k_cross(s):
        return remote(kr.at[s, OWN], kr.at[s, PART], kz_s.at[s], kz_r.at[s], partner)

    def k_far(s):
        return remote(kr.at[s, PART], kr.at[s, FAR], ky_s.at[s], ky_r.at[s], far_to)

    def k_frame(s, side, row):
        return remote(
            kr.at[s, row], kr.at[s, 3 * (2 - side) + row],
            kf_s.at[s, side, row], kf_r.at[s, 1 - side, row], sides[side][0],
        )

    def k_frame_in(s, side, row):
        return remote(
            kr.at[s, row], kr.at[s, 3 * (1 + side) + row],
            kf_s.at[s, side, row], kf_r.at[s, side, row], sides[side][0],
        )

    def g_frame(s, side, row):
        return remote(
            gp.at[s, 3 * (1 + side) + row], gf.at[s, 1 - side, row],
            gf_s.at[s, side, row], gf_r.at[s, 1 - side, row], sides[side][0],
        )

    def g_frame_in(s, side, row):
        return remote(
            gp.at[s, 3 * (1 + side) + row], gf.at[s, side, row],
            gf_s.at[s, side, row], gf_r.at[s, side, row], sides[side][0],
        )

    def g_far(s):
        return remote(gp.at[s, FAR], gy.at[s], gy_s.at[s], gy_r.at[s], far_from)

    def g_cross(s):
        return remote(gp.at[s, PART], gz.at[s], gz_s.at[s], gz_r.at[s], partner)

    def each_side(fn, extra=None):
        for side in range(2):
            cond = sides[side][1] if extra is None else sides[side][1] & extra

            @pl.when(cond)
            def _(side=side):
                fn(side)

    def row_exists(row):
        return has_from if row == FAR else None

    lane = lax.broadcasted_iota(jnp.int32, (2, 8, tile), 2)
    group = lax.broadcasted_iota(jnp.int32, (2, 8, tile), 0)
    cross_col = jnp.where(lax.rem(lane // TW, 2) != group, 1.0, 0.0)
    to_log2 = jnp.float32(LANES**-0.5 * LOG2E)

    def attend(s, tiles):
        head = meta[0, s]
        q = by_head[1, head]
        bias = cross_col * closed[2, s]
        top = None
        for n, t in enumerate([None] + tiles):
            keys = by_head[3, head] if t is None else kr[s, t]
            sc = dot(keys, q, 1, 1)
            if t is not None:
                limit = bias
                if t // 3:
                    limit = limit + closed[0, s] + jnp.where(sides[t // 3 - 1][1], 0.0, NEG)
                if t % 3:
                    limit = limit + closed[1, s]
                if t % 3 == FAR:
                    limit = limit + jnp.where(has_from, 0.0, NEG)
                sc = (sc.reshape(tile // 16, 2, 8, tile) + limit).reshape(tile, tile)
            s_ref[n * tile:(n + 1) * tile, :] = sc
            m = jnp.max(sc.reshape(tile // 8, 8, tile), axis=0)
            top = m if top is None else jnp.maximum(top, m)
        top = jnp.max(top, axis=0, keepdims=True)
        total = jnp.zeros((8, tile), jnp.float32)
        for n in range(len(tiles) + 1):
            e = jnp.exp2((s_ref[n * tile:(n + 1) * tile, :] - top) * to_log2)
            total = total + jnp.sum(e.reshape(tile // 8, 8, tile), axis=0)
            p_ref[n * tile:(n + 1) * tile, :] = e.astype(jnp.bfloat16)
        total = jnp.sum(total, axis=0, keepdims=True)
        inverse = jnp.transpose(jnp.broadcast_to(1.0 / total, (8, tile)))[:, :1]
        cot = (by_head[2, head].astype(jnp.float32) * inverse).astype(jnp.bfloat16)
        for n, t in enumerate([None] + tiles):
            g = dot(p_ref[n * tile:(n + 1) * tile, :], cot, 1, 0)
            if t is None:
                tvs[s] = g
            elif t < 3:
                ga[s, t] = g
            else:
                gp[s, t] = g.astype(jnp.bfloat16)

    def in_range(i, lo, hi, fn):
        if hi > lo:
            @pl.when((i >= lo) & (i < hi))
            def _():
                fn(i)

    def start_frames(s, row):
        each_side(lambda side: k_frame(s, side, row).start(), row_exists(row))

    def pass_partner(s):
        k_cross(s).wait_recv()

        @pl.when(has_to)
        def _():
            k_far(s).start()
        in_range(s, 0, n_a, lambda s: start_frames(s, PART))

    def pass_far(s):
        @pl.when(has_from)
        def _():
            k_far(s).wait_recv()
        in_range(s, 0, n_a, lambda s: start_frames(s, FAR))

    def frames_in(s, row_list):
        for row in row_list:
            each_side(lambda side: k_frame_in(s, side, row).wait_recv(), row_exists(row))

    def frames_out(s, row_list):
        for row in row_list:
            each_side(lambda side: g_frame(s, side, row).start(), row_exists(row))

    def compute_a(s):
        frames_in(s, range(3))
        attend(s, list(range(9)))
        frames_out(s, (FAR, PART, OWN))

    def compute_b(s):
        attend(s, [0, 1, 2])

    def compute_c(s):
        frames_in(s, [OWN])
        attend(s, [0, 3, 6])
        frames_out(s, [OWN])

    def add_frames(s, row):
        def add(side):
            g_frame_in(s, side, row).wait_recv()
            ga[s, row] = ga[s, row] + gf[s, side, row].astype(jnp.float32)
        each_side(add, row_exists(row))

    def reduce_far(s):
        in_range(s, 0, n_a, lambda s: add_frames(s, FAR))

        @pl.when(has_from)
        def _():
            gp[s, FAR] = ga[s, FAR].astype(jnp.bfloat16)
            g_far(s).start()

    def reduce_partner(s):
        in_range(s, 0, n_a, lambda s: add_frames(s, PART))

        @pl.when(has_to)
        def _():
            g_far(s).wait_recv()
            ga[s, PART] = ga[s, PART] + gy[s].astype(jnp.float32)
        gp[s, PART] = ga[s, PART].astype(jnp.bfloat16)
        g_cross(s).start()

    def finish(s):
        in_range(s, 0, n_a, lambda s: add_frames(s, OWN))
        in_range(s, n_rows, heads, lambda s: add_frames(s, OWN))
        if n_rows:
            @pl.when(s < n_rows)
            def _():
                g_cross(s).wait_recv()
                ga[s, OWN] = ga[s, OWN] + gz[s].astype(jnp.float32)
        vgs[s] = ga[s, OWN].astype(jnp.bfloat16)

    for s in range(min(AHEAD, n_rows)):
        k_cross(s).start()

    @pl.loop(0, heads)
    def _(s):
        in_range(s, 0, n_a, lambda s: start_frames(s, OWN))
        in_range(s, n_rows, heads, lambda s: start_frames(s, OWN))

    @pl.loop(0, heads + 6)
    def _(i):
        in_range(i + AHEAD, 0, n_rows, lambda s: k_cross(s).start())
        in_range(i, 0, n_rows, pass_partner)
        in_range(i - 1, 0, n_rows, pass_far)
        in_range(i - 2, 0, n_a, compute_a)
        in_range(i - 2, n_a, n_rows, compute_b)
        in_range(i - 2, n_rows, heads, compute_c)
        in_range(i - 3, 0, n_rows, reduce_far)
        in_range(i - 4, 0, n_rows, reduce_partner)
        in_range(i - 6, 0, heads, finish)

    for j in range(heads):
        slot = meta[1, j]
        vg_ref[:, j * LANES:(j + 1) * LANES] = vgs[slot]
        tv_ref[:, j * LANES:(j + 1) * LANES] = tvs[slot]

    @pl.loop(0, heads)
    def _(s):
        def sent_rows(s):
            k_cross(s).wait_send()
            g_cross(s).wait_send()

            @pl.when(has_to)
            def _():
                k_far(s).wait_send()

            @pl.when(has_from)
            def _():
                g_far(s).wait_send()

        def sent_frames(s, row_list):
            for row in row_list:
                each_side(lambda side: k_frame(s, side, row).wait_send(), row_exists(row))
                each_side(lambda side: g_frame(s, side, row).wait_send(), row_exists(row))
        in_range(s, 0, n_rows, sent_rows)
        in_range(s, 0, n_a, lambda s: sent_frames(s, range(3)))
        in_range(s, n_rows, heads, lambda s: sent_frames(s, [OWN]))


def attention(n_a, n_b, cid, frames, rows, meta, closed, q, k, c, tk):
    tile, width = k.shape
    heads = width // LANES
    vmem = pl.BlockSpec(memory_space=pltpu.VMEM)
    sem = pltpu.SemaphoreType.DMA
    bf, f32 = jnp.bfloat16, jnp.float32
    box = (tile, LANES)
    return pl.pallas_call(
        functools.partial(attention_kernel, n_a, n_b, heads, frames, rows),
        out_shape=(jax.ShapeDtypeStruct((tile, width), bf), jax.ShapeDtypeStruct((tile, width), f32)),
        in_specs=[pl.BlockSpec(memory_space=pltpu.SMEM)] * 2 + [vmem] * 4,
        out_specs=(vmem, vmem),
        scratch_shapes=[
            pltpu.VMEM((4, heads) + box, bf),
            pltpu.VMEM((heads, 9) + box, bf),
            pltpu.VMEM((heads, 9) + box, bf),
            pltpu.VMEM((heads, 3) + box, f32),
            pltpu.VMEM((heads, 2, 3) + box, bf),
            pltpu.VMEM((heads,) + box, bf),
            pltpu.VMEM((heads,) + box, bf),
            pltpu.VMEM((heads,) + box, bf),
            pltpu.VMEM((heads,) + box, f32),
            pltpu.VMEM((10 * tile, tile), f32),
            pltpu.VMEM((10 * tile, tile), bf),
            sem((heads,)), sem((heads,)), sem((heads,)), sem((heads,)),
            sem((heads, 2, 3)), sem((heads, 2, 3)), sem((heads, 2, 3)), sem((heads, 2, 3)),
            sem((heads,)), sem((heads,)), sem((heads,)), sem((heads,)),
        ],
        compiler_params=pltpu.CompilerParams(
            collective_id=cid, has_side_effects=True, vmem_limit_bytes=56 << 20
        ),
    )(meta, closed, q, k, c, tk)


def split2(x):
    hi = x.astype(jnp.bfloat16)
    return hi, (x - hi.astype(jnp.float32)).astype(jnp.bfloat16)


def sketch_kernel(
    token_total,
    time_ref, seed_ref, vg_ref, tv_ref, clean_ref, noise_ref, text_ref,
    di_ref, ui_ref, dt_ref, ut_ref, out_ref,
    flat, part, box1, box2, s_sem, r_sem,
):
    f = lax.axis_index("tm")
    h = lax.axis_index("height")
    g = 2 * f + lax.rem(h, 2)
    w = h // 2
    count = 16

    def in_ring(i):
        return (i // 2, 2 * w + lax.rem(i, 2))

    def in_plane(i):
        return (f, 2 * i + lax.rem(h, 2))

    barrier = pltpu.get_barrier_semaphore()

    @pl.loop(1, count)
    def _(k):
        pl.semaphore_signal(barrier, inc=1, device_id=in_ring(lax.rem(g + k, count)), device_id_type=MESH)
        pl.semaphore_signal(barrier, inc=1, device_id=in_plane(lax.rem(w + k, count)), device_id_type=MESH)

    width = vg_ref.shape[1]
    depth = clean_ref.shape[1]
    rank = ui_ref.shape[0]
    copies = LANES // rank
    level = jnp.full((1, depth), time_ref[0], jnp.int32).astype(jnp.float32) / 1000.0
    mixed = (
        (1.0 - level) * clean_ref[...].astype(jnp.float32) + level * noise_ref[...].astype(jnp.float32)
    ).astype(jnp.bfloat16)
    vg = vg_ref[...]
    hidden = dot(mixed, di_ref[...], 1, 1).astype(jnp.bfloat16)
    up_image = dot(hidden, vg, 0, 0)
    ui_wide = jnp.concatenate([ui_ref[...]] * copies, axis=0)
    ut_wide = jnp.concatenate([ut_ref[...]] * copies, axis=0)
    back = dot(vg, ui_wide, 1, 1).astype(jnp.bfloat16)
    lane8 = lax.broadcasted_iota(jnp.int32, (1, copies, LANES), 2)
    row8 = lax.broadcasted_iota(jnp.int32, (1, copies, LANES), 1)
    pick = lane8 // rank == row8

    def place_down(base, wide):
        kept = jnp.where(pick, wide.reshape(-1, copies, LANES), 0.0)
        flat[base:base + depth // copies, :] = jnp.sum(kept, axis=1)

    def place_up(base, grad):
        per = width // LANES
        for r in range(rank):
            for m in range(per):
                row = base + r * per + m
                flat[row:row + 1, :] = grad[r:r + 1, m * LANES:(m + 1) * LANES]

    place_down(0, dot(mixed, back, 0, 0))
    place_up(384, up_image)
    text = text_ref[...]
    tv_hi, tv_lo = split2(tv_ref[...])
    th_hi, th_lo = split2(dot(text, dt_ref[...], 1, 1))
    place_up(960, dot(th_hi, tv_hi, 0, 0) + (dot(th_hi, tv_lo, 0, 0) + dot(th_lo, tv_hi, 0, 0)))
    tb_hi, tb_lo = split2(dot(tv_hi, ut_wide, 1, 1) + dot(tv_lo, ut_wide, 1, 1))
    place_down(576, dot(text, tb_hi, 0, 0) + dot(text, tb_lo, 0, 0))

    total_rows = flat.shape[0]
    pos = lax.broadcasted_iota(jnp.int32, (total_rows, LANES), 0) * LANES
    pos = pos + lax.broadcasted_iota(jnp.int32, (total_rows, LANES), 1)
    bits = pos * 1103515245 + seed_ref[0] * 12345 + 1013904223
    bits = bits ^ (bits >> 16)
    bits = bits * 73244475
    bits = bits ^ (bits >> 16)
    signs = (1 - 2 * ((bits >> 7) & 1)).astype(jnp.float32)
    rows = SKETCH // LANES
    pieces = total_rows // rows
    scale = (token_total * pieces) ** -0.5
    signed = flat[...] * signs
    acc = signed[0:rows]
    for m in range(1, pieces):
        acc = acc + signed[m * rows:(m + 1) * rows]
    chunk = rows // count
    part[...] = (acc * scale).reshape(count, chunk, LANES)

    pl.semaphore_wait(barrier, 2 * (count - 1))

    def send1(k):
        i = lax.rem(g + k, count)
        return remote(part.at[i], box1.at[g], s_sem.at[0, k], r_sem.at[0, g], in_ring(i))

    def send2(k):
        i = lax.rem(w + k, count)
        return remote(box2.at[w], box2.at[w], s_sem.at[1, k], r_sem.at[1, w], in_plane(i))

    def send3(k):
        i = lax.rem(g + k, count)
        return remote(out_ref.at[g], out_ref.at[g], s_sem.at[2, k], r_sem.at[2, g], in_ring(i))

    def recv(phase, dst, i):
        return remote(dst.at[i], dst.at[i], s_sem.at[phase, 0], r_sem.at[phase, i], in_ring(lax.rem(g + 1, count)))

    def phase(n, me, dst, send):
        @pl.loop(1, count)
        def _(k):
            send(k).start()

        @pl.loop(1, count)
        def _(k):
            recv(n, dst, lax.rem(me + k, count)).wait_recv()

    box1[g] = part[g]
    phase(0, g, box1, send1)
    box2[w] = jnp.sum(box1[...], axis=0)
    phase(1, w, box2, send2)
    out_ref[g] = jnp.sum(box2[...], axis=0)
    phase(2, g, out_ref, send3)

    @pl.loop(1, count)
    def _(k):
        send1(k).wait_send()
        send2(k).wait_send()
        send3(k).wait_send()


def sketch(cid, token_total, *args):
    vmem = pl.BlockSpec(memory_space=pltpu.VMEM)
    smem = pl.BlockSpec(memory_space=pltpu.SMEM)
    rows = SKETCH // LANES
    f32 = jnp.float32
    return pl.pallas_call(
        functools.partial(sketch_kernel, token_total),
        out_shape=jax.ShapeDtypeStruct((16, rows // 16, LANES), f32),
        in_specs=[smem, smem] + [vmem] * 9,
        out_specs=vmem,
        scratch_shapes=[
            pltpu.VMEM((9 * rows, LANES), f32),
            pltpu.VMEM((16, rows // 16, LANES), f32),
            pltpu.VMEM((16, rows // 16, LANES), f32),
            pltpu.VMEM((16, rows // 16, LANES), f32),
            pltpu.SemaphoreType.DMA((3, 16)),
            pltpu.SemaphoreType.DMA((3, 16)),
        ],
        compiler_params=pltpu.CompilerParams(
            collective_id=cid, has_side_effects=True, vmem_limit_bytes=56 << 20
        ),
    )(*args)


VARIANTS = ((2, 3), (3, 3), (4, 3), (5, 3), (7, 2), (12, 0))


def plan_kernel(variants, heads, radii, choice, meta, closed):
    kinds = []
    counts = [jnp.int32(0)] * 4
    ranks = []
    for j in range(heads):
        far_f, far_r = radii[j, 0] > 0, radii[j, 1] > 0
        kind = jnp.where(far_r, jnp.where(far_f, 0, 1), jnp.where(far_f, 2, 3))
        kinds.append(kind)
        rank = jnp.int32(0)
        for t in range(4):
            rank = jnp.where(kind == t, counts[t], rank)
            counts[t] = counts[t] + jnp.where(kind == t, 1, 0)
        ranks.append(rank)
    pick = jnp.int32(len(variants) - 1)
    a, b = jnp.int32(variants[-1][0]), jnp.int32(variants[-1][1])
    for i in reversed(range(len(variants) - 1)):
        va, vb = variants[i]
        vc = heads - va - vb
        fits = (counts[0] <= va) & (counts[0] + counts[1] <= va + vb) & (counts[0] + counts[2] <= va + vc)
        pick = jnp.where(fits, i, pick)
        a, b = jnp.where(fits, va, a), jnp.where(fits, vb, b)
    c = heads - a - b
    over_b = jnp.maximum(counts[1] - b, 0)
    over_c = jnp.maximum(counts[2] - c, 0)
    spare_a = a - counts[0] - over_b - over_c
    spare_b = b - (counts[1] - over_b)
    choice[0] = pick
    for j in range(heads):
        kind, rank = kinds[j], ranks[j]
        slot_b = jnp.where(rank < over_b, counts[0] + rank, a + rank - over_b)
        slot_c = jnp.where(rank < over_c, counts[0] + over_b + rank, heads - counts[2] + rank)
        left = rank - spare_a - spare_b
        slot_d = jnp.where(
            rank < spare_a,
            counts[0] + over_b + over_c + rank,
            a + b + left,
        )
        slot = jnp.where(kind == 0, rank, jnp.where(kind == 1, slot_b, jnp.where(kind == 2, slot_c, slot_d)))
        meta[0, slot] = j
        meta[1, j] = slot
        for r in range(3):
            closed[r, slot] = jnp.where(radii[j, r] > 0, 0.0, NEG)


def plan(radii):
    heads = radii.shape[0]
    smem = pl.BlockSpec(memory_space=pltpu.SMEM)
    return pl.pallas_call(
        functools.partial(plan_kernel, VARIANTS, heads),
        out_shape=(
            jax.ShapeDtypeStruct((1,), jnp.int32),
            jax.ShapeDtypeStruct((2, heads), jnp.int32),
            jax.ShapeDtypeStruct((3, heads), jnp.float32),
        ),
        in_specs=[smem],
        out_specs=(smem, smem, smem),
    )(radii)


def per_device(
    clean_latents, gaussian_noise, text_states, queries, key_states, cotangent, text_keys,
    window_radii, timestep, sketch_seed, down_image, up_image, down_text, up_text,
):
    width = queries.shape[-1]
    depth = clean_latents.shape[-1]
    frames, rows = lax.axis_size("tm"), lax.axis_size("height")
    choice, meta, closed = plan(window_radii)
    branches = [
        functools.partial(attention, a, b, i + 1, frames, rows) for i, (a, b) in enumerate(VARIANTS)
    ]
    operands = (
        meta,
        closed,
        queries.reshape(-1, width),
        key_states.reshape(-1, width),
        cotangent.reshape(-1, width),
        text_keys,
    )
    if len(branches) == 1:
        vg, tv = branches[0](*operands)
    else:
        vg, tv = lax.switch(choice[0], branches, *operands)
    tokens = vg.shape[0] * frames * rows
    sk = sketch(
        0, tokens, timestep, sketch_seed, vg, tv,
        clean_latents.reshape(-1, depth), gaussian_noise.reshape(-1, depth), text_states,
        down_image.T, up_image, down_text.T, up_text,
    )
    return vg.reshape(queries.shape), sk.reshape(-1)


def solution(mesh):
    block = P("tm", "height", None, None)
    return jax.shard_map(
        per_device,
        mesh=mesh,
        in_specs=(block, block, P(), block, block, block) + (P(),) * 8,
        out_specs=(block, P()),
        check_vma=False,
    )
```

```python
import functools

import jax
import jax.numpy as jnp
from jax import lax
from jax.experimental import pallas as pl
from jax.experimental.pallas import tpu as pltpu
from jax.sharding import PartitionSpec as P

MESH = pl.DeviceIdType.MESH
TW = 8
LANES = 128
SKETCH = 16384
NEG = -1e30
LOG2E = 1.4426950408889634
OWN, PART, FAR = 0, 1, 2
AHEAD = 3


def dot(a, b, ca, cb):
    return lax.dot_general(a, b, (((ca,), (cb,)), ((), ())), preferred_element_type=jnp.float32)


def remote(src, dst, ssem, rsem, device):
    return pltpu.make_async_remote_copy(
        src_ref=src, dst_ref=dst, send_sem=ssem, recv_sem=rsem, device_id=device, device_id_type=MESH
    )


def attention_kernel(
    n_a, n_b, heads, frames, rows, token_total,
    meta, closed, time_ref, seed_ref, k_ref, ui_ref, ut_ref, di_ref, dt_ref,
    q_hbm, c_hbm, tk_hbm, clean_hbm, noise_hbm, text_hbm, vg_ref, out_ref,
    q_ref, c_ref, tk_ref, clean_ref, noise_ref, text_ref, l_sem,
    mixed_t, hid_t, text_hid, ui_wide, back, up_s, flat, signs, part, box1, box2, a_s, a_r,
    by_head, kr, gp, ga, gf, gy, gz, vgs, tvs, s_ref, p_ref,
    kz_s, kz_r, ky_s, ky_r, kf_s, kf_r, gf_s, gf_r, gy_s, gy_r, gz_s, gz_r,
):
    n_rows = n_a + n_b
    tile = k_ref.shape[0]
    f = lax.axis_index("tm")
    h = lax.axis_index("height")
    even = lax.rem(h, 2) == 0
    partner = (f, h + 1 - 2 * lax.rem(h, 2))
    step = 2 - 4 * lax.rem(h, 2)
    has_to = (h + step >= 0) & (h + step < rows)
    has_from = (h - step >= 0) & (h - step < rows)
    far_to = (f, jnp.where(has_to, h + step, h))
    far_from = (f, jnp.where(has_from, h - step, h))
    has_low = f > 0
    has_high = f < frames - 1
    low = (jnp.maximum(f - 1, 0), h)
    high = (jnp.minimum(f + 1, frames - 1), h)
    sides = ((low, has_low), (high, has_high))

    g = 2 * f + lax.rem(h, 2)
    w = h // 2
    count = 16

    def in_ring(i):
        return (i // 2, 2 * w + lax.rem(i, 2))

    def in_plane(i):
        return (f, 2 * i + lax.rem(h, 2))

    barrier = pltpu.get_barrier_semaphore()

    @pl.loop(1, count)
    def _(k):
        pl.semaphore_signal(barrier, inc=1, device_id=in_ring(lax.rem(g + k, count)), device_id_type=MESH)
        pl.semaphore_signal(barrier, inc=1, device_id=in_plane(lax.rem(w + k, count)), device_id_type=MESH)

    loads = [
        pltpu.make_async_copy(src, dst, l_sem.at[n])
        for n, (src, dst) in enumerate((
            (q_hbm, q_ref), (c_hbm, c_ref), (tk_hbm, tk_ref),
            (clean_hbm, clean_ref), (noise_hbm, noise_ref), (text_hbm, text_ref),
        ))
    ]
    for load in loads:
        load.start()

    def columns(j, size=LANES):
        return pl.ds(pl.multiple_of(j * size, size), size)

    @pl.loop(0, heads)
    def _(j):
        by_head[0, j] = k_ref[:, columns(j)]

    @pl.loop(0, heads)
    def _(s):
        kr[s, 0] = by_head[0, meta[0, s]]

    for side, exists in enumerate((has_low, has_high)):
        @pl.when(jnp.logical_not(exists))
        def _(side=side):
            @pl.loop(0, heads)
            def _(s):
                for row in range(3):
                    kr[s, 3 * (1 + side) + row] = jnp.zeros((tile, LANES), jnp.bfloat16)

    @pl.when(jnp.logical_not(has_from))
    def _():
        @pl.loop(0, heads)
        def _(s):
            for t in (FAR, 3 + FAR, 6 + FAR):
                kr[s, t] = jnp.zeros((tile, LANES), jnp.bfloat16)

    pl.semaphore_wait(barrier, 2 * (count - 1))

    def k_cross(s):
        return remote(kr.at[s, OWN], kr.at[s, PART], kz_s.at[s], kz_r.at[s], partner)

    def k_far(s):
        return remote(kr.at[s, PART], kr.at[s, FAR], ky_s.at[s], ky_r.at[s], far_to)

    def k_frame(s, side, row):
        return remote(
            kr.at[s, row], kr.at[s, 3 * (2 - side) + row],
            kf_s.at[s, side, row], kf_r.at[s, 1 - side, row], sides[side][0],
        )

    def k_frame_in(s, side, row):
        return remote(
            kr.at[s, row], kr.at[s, 3 * (1 + side) + row],
            kf_s.at[s, side, row], kf_r.at[s, side, row], sides[side][0],
        )

    def g_frame(s, side, row):
        return remote(
            gp.at[s, 3 * (1 + side) + row], gf.at[s, 1 - side, row],
            gf_s.at[s, side, row], gf_r.at[s, 1 - side, row], sides[side][0],
        )

    def g_frame_in(s, side, row):
        return remote(
            gp.at[s, 3 * (1 + side) + row], gf.at[s, side, row],
            gf_s.at[s, side, row], gf_r.at[s, side, row], sides[side][0],
        )

    def g_far(s):
        return remote(gp.at[s, FAR], gy.at[s], gy_s.at[s], gy_r.at[s], far_from)

    def g_cross(s):
        return remote(gp.at[s, PART], gz.at[s], gz_s.at[s], gz_r.at[s], partner)

    def each_side(fn, extra=None):
        for side in range(2):
            cond = sides[side][1] if extra is None else sides[side][1] & extra

            @pl.when(cond)
            def _(side=side):
                fn(side)

    def row_exists(row):
        return has_from if row == FAR else None

    lane = lax.broadcasted_iota(jnp.int32, (2, 8, tile), 2)
    group = lax.broadcasted_iota(jnp.int32, (2, 8, tile), 0)
    cross_col = jnp.where(lax.rem(lane // TW, 2) != group, 1.0, 0.0)
    to_log2 = jnp.float32(LANES**-0.5 * LOG2E)

    def attend(s, tiles):
        head = meta[0, s]
        q = by_head[1, head]
        bias = cross_col * closed[2, s]
        low_limit = closed[0, s] + jnp.where(has_low, 0.0, NEG)
        high_limit = closed[0, s] + jnp.where(has_high, 0.0, NEG)
        far_limit = closed[1, s] + jnp.where(has_from, 0.0, NEG)
        stride, number = tiles

        def score(n, keys, limit, top):
            sc = dot(keys, q, 1, 1)
            if limit is not None:
                sc = (sc.reshape(tile // 16, 2, 8, tile) + limit).reshape(tile, tile)
            s_ref[n] = sc
            return jnp.maximum(top, jnp.max(sc.reshape(tile // 8, 8, tile), axis=0))

        def score_tile(n, top):
            t = n * stride
            limit = bias
            if t // 3:
                limit = limit + (low_limit, high_limit)[t // 3 - 1]
            if t % 3:
                limit = limit + (closed[1, s], far_limit)[t % 3 - 1]
            return score(n, kr[s, t], limit, top)

        top = score(number, by_head[3, head], None, jnp.full((8, tile), NEG, jnp.float32))
        for n in range(number):
            top = score_tile(n, top)
        top = jnp.max(top, axis=0, keepdims=True)

        def weigh(n, total):
            e = jnp.exp2((s_ref[n] - top) * to_log2)
            p_ref[n] = e.astype(jnp.bfloat16)
            return total + jnp.sum(e.reshape(tile // 8, 8, tile), axis=0)

        total = jnp.zeros((8, tile), jnp.float32)
        for n in range(number + 1):
            total = weigh(n, total)
        total = jnp.sum(total, axis=0, keepdims=True)
        inverse = jnp.transpose(jnp.broadcast_to(1.0 / total, (8, tile)))[:, :1]
        cot = (by_head[2, head].astype(jnp.float32) * inverse).astype(jnp.bfloat16)
        tvs[s] = dot(p_ref[number], cot, 1, 0)

        for n in range(number):
            t = n * stride
            grad = dot(p_ref[n], cot, 1, 0)
            if t < 3:
                ga[s, t] = grad
            else:
                gp[s, t] = grad.astype(jnp.bfloat16)

    def in_range(i, lo, hi, fn):
        if hi > lo:
            @pl.when((i >= lo) & (i < hi))
            def _():
                fn(i)

    def start_frames(s, row):
        each_side(lambda side: k_frame(s, side, row).start(), row_exists(row))

    def pass_partner(s):
        k_cross(s).wait_recv()

        @pl.when(has_to)
        def _():
            k_far(s).start()
        in_range(s, 0, n_a, lambda s: start_frames(s, PART))

    def pass_far(s):
        @pl.when(has_from)
        def _():
            k_far(s).wait_recv()
        in_range(s, 0, n_a, lambda s: start_frames(s, FAR))

    def frames_in(s, row_list):
        for row in row_list:
            each_side(lambda side: k_frame_in(s, side, row).wait_recv(), row_exists(row))

    def frames_out(s, row_list):
        for row in row_list:
            each_side(lambda side: g_frame(s, side, row).start(), row_exists(row))

    def compute_a(s):
        frames_in(s, range(3))
        attend(s, (1, 9))
        frames_out(s, (FAR, PART, OWN))

    def compute_b(s):
        attend(s, (1, 3))

    def compute_c(s):
        frames_in(s, [OWN])
        attend(s, (3, 3))
        frames_out(s, [OWN])

    def add_frames(s, row):
        def add(side):
            g_frame_in(s, side, row).wait_recv()
            ga[s, row] = ga[s, row] + gf[s, side, row].astype(jnp.float32)
        each_side(add, row_exists(row))

    def reduce_far(s):
        in_range(s, 0, n_a, lambda s: add_frames(s, FAR))

        @pl.when(has_from)
        def _():
            gp[s, FAR] = ga[s, FAR].astype(jnp.bfloat16)
            g_far(s).start()

    def reduce_partner(s):
        in_range(s, 0, n_a, lambda s: add_frames(s, PART))

        @pl.when(has_to)
        def _():
            g_far(s).wait_recv()
            ga[s, PART] = ga[s, PART] + gy[s].astype(jnp.float32)
        gp[s, PART] = ga[s, PART].astype(jnp.bfloat16)
        g_cross(s).start()

    def finish(s):
        in_range(s, 0, n_a, lambda s: add_frames(s, OWN))
        in_range(s, n_rows, heads, lambda s: add_frames(s, OWN))
        if n_rows:
            @pl.when(s < n_rows)
            def _():
                g_cross(s).wait_recv()
                ga[s, OWN] = ga[s, OWN] + gz[s].astype(jnp.float32)
        grad = ga[s, OWN].astype(jnp.bfloat16)
        vgs[s] = grad
        up_s[s] = dot(hid_t[...], grad, 1, 0)
        back[...] = back[...] + dot(grad, ui_wide[meta[0, s]], 1, 1)

    for s in range(min(AHEAD, n_rows)):
        k_cross(s).start()

    @pl.loop(0, heads)
    def _(s):
        in_range(s, 0, n_a, lambda s: start_frames(s, OWN))
        in_range(s, n_rows, heads, lambda s: start_frames(s, OWN))

    depth = clean_ref.shape[1]
    rank = ui_ref.shape[0]
    copies = LANES // rank
    per = heads
    lane8 = lax.broadcasted_iota(jnp.int32, (1, copies, LANES), 2)
    row8 = lax.broadcasted_iota(jnp.int32, (1, copies, LANES), 1)
    pick = lane8 // rank == row8

    block = 512
    blocks = depth // block
    sketch_rows = SKETCH // LANES
    pieces = flat.shape[0] // sketch_rows

    def place_down(base, n, wide):
        kept = jnp.where(pick, wide.reshape(-1, copies, LANES), 0.0)
        flat[pl.ds(pl.multiple_of(base + n * (block // copies), 64), block // copies), :] = jnp.sum(kept, axis=1)

    def place_up(base, m, grad):
        for r in range(rank):
            flat[pl.ds(base + r * per + m, 1), :] = grad[r:r + 1, :]

    for n, ref in enumerate((q_ref, c_ref, tk_ref)):
        loads[n].wait()

        @pl.loop(0, heads)
        def _(j):
            by_head[n + 1, j] = ref[:, columns(j)]

    @pl.loop(0, heads)
    def _(j):
        ui_wide[j] = jnp.concatenate([ui_ref[:, columns(j)]] * copies, axis=0)

    back[...] = jnp.zeros_like(back)
    for n in range(3, 6):
        loads[n].wait()
    level = jnp.full((1, block), time_ref[0], jnp.int32).astype(jnp.float32) / 1000.0

    def mix(n, hid):
        cols = columns(n, block)
        mixed = (
            (1.0 - level) * clean_ref[:, cols].astype(jnp.float32)
            + level * noise_ref[:, cols].astype(jnp.float32)
        ).astype(jnp.bfloat16)
        mixed_t[n] = jnp.transpose(mixed)
        return hid + dot(di_ref[:, cols], mixed, 1, 1)

    hid_t[...] = lax.fori_loop(0, blocks, mix, jnp.zeros((rank, tile), jnp.float32)).astype(jnp.bfloat16)
    text_hid[...] = dot(dt_ref[...], text_ref[...], 1, 1)

    @pl.loop(0, pieces)
    def _(m):
        pos = lax.broadcasted_iota(jnp.int32, (sketch_rows, LANES), 0) * LANES
        pos = pos + lax.broadcasted_iota(jnp.int32, (sketch_rows, LANES), 1) + m * SKETCH
        bits = pos * 1103515245 + seed_ref[0] * 12345 + 1013904223
        bits = bits ^ (bits >> 16)
        bits = bits * 73244475
        bits = bits ^ (bits >> 16)
        signs[m] = (1 - 2 * ((bits >> 7) & 1)).astype(jnp.float32)

    def text_grads():
        th_hi, th_lo = split2(text_hid[...])

        def per_head(j, text_back):
            tv_hi, tv_lo = split2(tvs[meta[1, j]])
            place_up(960, j, dot(th_hi, tv_hi, 1, 0) + (dot(th_hi, tv_lo, 1, 0) + dot(th_lo, tv_hi, 1, 0)))
            cols = jnp.concatenate([ut_ref[:, columns(j)]] * copies, axis=0)
            return text_back + (dot(tv_hi, cols, 1, 1) + dot(tv_lo, cols, 1, 1))

        text_back = lax.fori_loop(0, heads, per_head, jnp.zeros((tile, LANES), jnp.float32))
        tb_hi, tb_lo = split2(text_back)

        @pl.loop(0, blocks)
        def _(n):
            text = text_ref[:, columns(n, block)]
            place_down(576, n, dot(text, tb_hi, 0, 0) + dot(text, tb_lo, 0, 0))

    @pl.loop(0, heads + 6)
    def _(i):
        in_range(i + AHEAD, 0, n_rows, lambda s: k_cross(s).start())
        in_range(i, 0, n_rows, pass_partner)
        in_range(i - 1, 0, n_rows, pass_far)
        in_range(i - 2, 0, n_a, compute_a)
        in_range(i - 2, n_a, n_rows, compute_b)
        in_range(i - 2, n_rows, heads, compute_c)
        in_range(i - 3, 0, n_rows, reduce_far)
        in_range(i - 4, 0, n_rows, reduce_partner)
        in_range(i, heads + 2, heads + 3, lambda i: text_grads())
        in_range(i - 6, 0, heads, finish)

    @pl.loop(0, heads)
    def _(j):
        slot = meta[1, j]
        vg_ref[:, columns(j)] = vgs[slot]
        place_up(384, j, up_s[slot])

    low_back = back[...].astype(jnp.bfloat16)

    @pl.loop(0, blocks)
    def _(n):
        place_down(0, n, dot(mixed_t[n], low_back, 1, 0))

    acc = flat[0:sketch_rows] * signs[0]
    for m in range(1, pieces):
        acc = acc + flat[m * sketch_rows:(m + 1) * sketch_rows] * signs[m]
    part[...] = (acc * (token_total * pieces) ** -0.5).reshape(count, sketch_rows // count, LANES)

    def send1(k):
        i = lax.rem(g + k, count)
        return remote(part.at[i], box1.at[g], a_s.at[0, k], a_r.at[0, g], in_ring(i))

    def send2(k):
        i = lax.rem(w + k, count)
        return remote(box2.at[w], box2.at[w], a_s.at[1, k], a_r.at[1, w], in_plane(i))

    def send3(k):
        i = lax.rem(g + k, count)
        return remote(out_ref.at[g], out_ref.at[g], a_s.at[2, k], a_r.at[2, g], in_ring(i))

    def recv(phase, dst, i):
        return remote(dst.at[i], dst.at[i], a_s.at[phase, 0], a_r.at[phase, i], in_ring(lax.rem(g + 1, count)))

    def phase(n, me, dst, send):
        @pl.loop(1, count)
        def _(k):
            send(k).start()

        @pl.loop(1, count)
        def _(k):
            recv(n, dst, lax.rem(me + k, count)).wait_recv()

    box1[g] = part[g]
    phase(0, g, box1, send1)
    box2[w] = jnp.sum(box1[...], axis=0)
    phase(1, w, box2, send2)
    out_ref[g] = jnp.sum(box2[...], axis=0)
    phase(2, g, out_ref, send3)

    @pl.loop(1, count)
    def _(k):
        send1(k).wait_send()
        send2(k).wait_send()
        send3(k).wait_send()

    @pl.loop(0, heads)
    def _(s):
        def sent_rows(s):
            k_cross(s).wait_send()
            g_cross(s).wait_send()

            @pl.when(has_to)
            def _():
                k_far(s).wait_send()

            @pl.when(has_from)
            def _():
                g_far(s).wait_send()

        def sent_frames(s, row_list):
            for row in row_list:
                each_side(lambda side: k_frame(s, side, row).wait_send(), row_exists(row))
                each_side(lambda side: g_frame(s, side, row).wait_send(), row_exists(row))
        in_range(s, 0, n_rows, sent_rows)
        in_range(s, 0, n_a, lambda s: sent_frames(s, range(3)))
        in_range(s, n_rows, heads, lambda s: sent_frames(s, [OWN]))


def attention(n_a, n_b, cid, frames, rows, *args):
    tile, width = args[4].shape
    depth = args[12].shape[1]
    rank = args[5].shape[0]
    lines = SKETCH // LANES
    heads = width // LANES
    vmem = pl.BlockSpec(memory_space=pltpu.VMEM)
    sem = pltpu.SemaphoreType.DMA
    bf, f32 = jnp.bfloat16, jnp.float32
    box = (tile, LANES)
    return pl.pallas_call(
        functools.partial(attention_kernel, n_a, n_b, heads, frames, rows, tile * frames * rows),
        out_shape=(jax.ShapeDtypeStruct((tile, width), bf), jax.ShapeDtypeStruct((16, lines // 16, LANES), f32)),
        in_specs=[pl.BlockSpec(memory_space=pltpu.SMEM)] * 4 + [vmem] * 5 + [pl.BlockSpec(memory_space=pl.ANY)] * 6,
        out_specs=(vmem, vmem),
        scratch_shapes=[
            pltpu.VMEM((tile, width), bf), pltpu.VMEM((tile, width), bf), pltpu.VMEM((tile, width), bf),
            pltpu.VMEM((tile, depth), bf), pltpu.VMEM((tile, depth), bf), pltpu.VMEM((tile, depth), bf),
            sem((6,)),
            pltpu.VMEM((depth // 512, 512, tile), bf),
            pltpu.VMEM((rank, tile), bf),
            pltpu.VMEM((rank, tile), f32),
            pltpu.VMEM((heads, LANES, LANES), bf),
            pltpu.VMEM((tile, LANES), f32),
            pltpu.VMEM((heads, rank, LANES), f32),
            pltpu.VMEM((9 * lines, LANES), f32),
            pltpu.VMEM((9, lines, LANES), f32),
            pltpu.VMEM((16, lines // 16, LANES), f32),
            pltpu.VMEM((16, lines // 16, LANES), f32),
            pltpu.VMEM((16, lines // 16, LANES), f32),
            sem((3, 16)), sem((3, 16)),
            pltpu.VMEM((4, heads) + box, bf),
            pltpu.VMEM((heads, 9) + box, bf),
            pltpu.VMEM((heads, 9) + box, bf),
            pltpu.VMEM((heads, 3) + box, f32),
            pltpu.VMEM((heads, 2, 3) + box, bf),
            pltpu.VMEM((heads,) + box, bf),
            pltpu.VMEM((heads,) + box, bf),
            pltpu.VMEM((heads,) + box, bf),
            pltpu.VMEM((heads,) + box, f32),
            pltpu.VMEM((10, tile, tile), f32),
            pltpu.VMEM((10, tile, tile), bf),
            sem((heads,)), sem((heads,)), sem((heads,)), sem((heads,)),
            sem((heads, 2, 3)), sem((heads, 2, 3)), sem((heads, 2, 3)), sem((heads, 2, 3)),
            sem((heads,)), sem((heads,)), sem((heads,)), sem((heads,)),
        ],
        compiler_params=pltpu.CompilerParams(
            collective_id=cid, has_side_effects=True, vmem_limit_bytes=56 << 20
        ),
    )(*args)


def split2(x):
    hi = x.astype(jnp.bfloat16)
    return hi, (x - hi.astype(jnp.float32)).astype(jnp.bfloat16)


VARIANTS = ((2, 3), (3, 3), (4, 3), (5, 3), (7, 2), (12, 0))


def plan_kernel(variants, heads, radii, choice, meta, closed):
    kinds = []
    counts = [jnp.int32(0)] * 4
    ranks = []
    for j in range(heads):
        far_f, far_r = radii[j, 0] > 0, radii[j, 1] > 0
        kind = jnp.where(far_r, jnp.where(far_f, 0, 1), jnp.where(far_f, 2, 3))
        kinds.append(kind)
        rank = jnp.int32(0)
        for t in range(4):
            rank = jnp.where(kind == t, counts[t], rank)
            counts[t] = counts[t] + jnp.where(kind == t, 1, 0)
        ranks.append(rank)
    pick = jnp.int32(len(variants) - 1)
    a, b = jnp.int32(variants[-1][0]), jnp.int32(variants[-1][1])
    for i in reversed(range(len(variants) - 1)):
        va, vb = variants[i]
        vc = heads - va - vb
        fits = (counts[0] <= va) & (counts[0] + counts[1] <= va + vb) & (counts[0] + counts[2] <= va + vc)
        pick = jnp.where(fits, i, pick)
        a, b = jnp.where(fits, va, a), jnp.where(fits, vb, b)
    c = heads - a - b
    over_b = jnp.maximum(counts[1] - b, 0)
    over_c = jnp.maximum(counts[2] - c, 0)
    spare_a = a - counts[0] - over_b - over_c
    spare_b = b - (counts[1] - over_b)
    choice[0] = pick
    for j in range(heads):
        kind, rank = kinds[j], ranks[j]
        slot_b = jnp.where(rank < over_b, counts[0] + rank, a + rank - over_b)
        slot_c = jnp.where(rank < over_c, counts[0] + over_b + rank, heads - counts[2] + rank)
        left = rank - spare_a - spare_b
        slot_d = jnp.where(
            rank < spare_a,
            counts[0] + over_b + over_c + rank,
            a + b + left,
        )
        slot = jnp.where(kind == 0, rank, jnp.where(kind == 1, slot_b, jnp.where(kind == 2, slot_c, slot_d)))
        meta[0, slot] = j
        meta[1, j] = slot
        for r in range(3):
            closed[r, slot] = jnp.where(radii[j, r] > 0, 0.0, NEG)


def plan(radii):
    heads = radii.shape[0]
    smem = pl.BlockSpec(memory_space=pltpu.SMEM)
    return pl.pallas_call(
        functools.partial(plan_kernel, VARIANTS, heads),
        out_shape=(
            jax.ShapeDtypeStruct((1,), jnp.int32),
            jax.ShapeDtypeStruct((2, heads), jnp.int32),
            jax.ShapeDtypeStruct((3, heads), jnp.float32),
        ),
        in_specs=[smem],
        out_specs=(smem, smem, smem),
    )(radii)


def per_device(
    clean_latents, gaussian_noise, text_states, queries, key_states, cotangent, text_keys,
    window_radii, timestep, sketch_seed, down_image, up_image, down_text, up_text,
):
    width = queries.shape[-1]
    depth = clean_latents.shape[-1]
    frames, rows = lax.axis_size("tm"), lax.axis_size("height")
    choice, meta, closed = plan(window_radii)
    branches = [
        functools.partial(attention, a, b, i + 1, frames, rows) for i, (a, b) in enumerate(VARIANTS)
    ]
    operands = (
        meta, closed, timestep, sketch_seed,
        key_states.reshape(-1, width), up_image, up_text, down_image.T, down_text.T,
        queries.reshape(-1, width), cotangent.reshape(-1, width), text_keys,
        clean_latents.reshape(-1, depth), gaussian_noise.reshape(-1, depth), text_states,
    )
    if len(branches) == 1:
        vg, sk = branches[0](*operands)
    else:
        vg, sk = lax.switch(choice[0], branches, *operands)
    return vg.reshape(queries.shape), sk.reshape(-1)


def solution(mesh):
    block = P("tm", "height", None, None)
    return jax.shard_map(
        per_device,
        mesh=mesh,
        in_specs=(block, block, P(), block, block, block) + (P(),) * 8,
        out_specs=(block, P()),
        check_vma=False,
    )
```

```python
import functools

import jax
import jax.numpy as jnp
from jax import lax
from jax.experimental import pallas as pl
from jax.experimental.pallas import tpu as pltpu
from jax.sharding import PartitionSpec as P

MESH = pl.DeviceIdType.MESH
TW = 8
LANES = 128
SKETCH = 16384
NEG = -1e30
LOG2E = 1.4426950408889634
OWN, PART, FAR = 0, 1, 2
AHEAD = 1


def dot(a, b, ca, cb):
    return lax.dot_general(a, b, (((ca,), (cb,)), ((), ())), preferred_element_type=jnp.float32)


def remote(src, dst, ssem, rsem, device):
    return pltpu.make_async_remote_copy(
        src_ref=src, dst_ref=dst, send_sem=ssem, recv_sem=rsem, device_id=device, device_id_type=MESH
    )


def attention_kernel(
    n_a, n_b, heads, frames, rows, token_total,
    meta, closed, time_ref, seed_ref, k_ref, ui_ref, ut_ref, di_ref, dt_ref,
    q_hbm, c_hbm, tk_hbm, clean_hbm, noise_hbm, text_hbm, vg_ref, out_ref,
    q_ref, c_ref, tk_ref, clean_ref, noise_ref, text_ref, l_sem,
    mixed_t, hid_t, text_hid, ui_wide, back, up_s, flat, signs, part, box1, box2, a_s, a_r,
    by_head, kr, gp, ga, gf, gy, gz, vgs, tvs, s_ref, p_ref,
    kz_s, kz_r, ky_s, ky_r, kf_s, kf_r, gf_s, gf_r, gy_s, gy_r, gz_s, gz_r,
):
    n_rows = n_a + n_b
    tile = k_ref.shape[0]
    f = lax.axis_index("tm")
    h = lax.axis_index("height")
    even = lax.rem(h, 2) == 0
    partner = (f, h + 1 - 2 * lax.rem(h, 2))
    step = 2 - 4 * lax.rem(h, 2)
    has_to = (h + step >= 0) & (h + step < rows)
    has_from = (h - step >= 0) & (h - step < rows)
    far_to = (f, jnp.where(has_to, h + step, h))
    far_from = (f, jnp.where(has_from, h - step, h))
    has_low = f > 0
    has_high = f < frames - 1
    low = (jnp.maximum(f - 1, 0), h)
    high = (jnp.minimum(f + 1, frames - 1), h)
    sides = ((low, has_low), (high, has_high))
    odd = lax.rem(f, 2)
    has_outer = jnp.where(odd == 1, f < frames - 1, f > 0)
    outer_f = jnp.where(has_outer, f - 1 + 2 * odd, f)
    outer = (outer_f, h)
    across = (outer_f, partner[1])
    inner = (f + 1 - 2 * odd, h)
    outer_side, inner_side = odd, 1 - odd
    outer_tile = 3 * (1 + odd)
    inner_tile = 3 * (2 - odd)

    g = 2 * f + lax.rem(h, 2)
    w = h // 2
    count = 16

    def in_ring(i):
        return (i // 2, 2 * w + lax.rem(i, 2))

    def in_plane(i):
        return (f, 2 * i + lax.rem(h, 2))

    barrier = pltpu.get_barrier_semaphore()

    @pl.loop(1, count)
    def _(k):
        pl.semaphore_signal(barrier, inc=1, device_id=in_ring(lax.rem(g + k, count)), device_id_type=MESH)
        pl.semaphore_signal(barrier, inc=1, device_id=in_plane(lax.rem(w + k, count)), device_id_type=MESH)

    loads = [
        pltpu.make_async_copy(src, dst, l_sem.at[n])
        for n, (src, dst) in enumerate((
            (q_hbm, q_ref), (c_hbm, c_ref), (tk_hbm, tk_ref),
            (clean_hbm, clean_ref), (noise_hbm, noise_ref), (text_hbm, text_ref),
        ))
    ]
    for load in loads:
        load.start()

    def columns(j, size=LANES):
        return pl.ds(pl.multiple_of(j * size, size), size)

    @pl.loop(0, heads)
    def _(j):
        by_head[0, j] = k_ref[:, columns(j)]

    @pl.loop(0, heads)
    def _(s):
        kr[s, 0] = by_head[0, meta[0, s]]

    for side, exists in enumerate((has_low, has_high)):
        @pl.when(jnp.logical_not(exists))
        def _(side=side):
            @pl.loop(0, heads)
            def _(s):
                for row in range(3):
                    kr[s, 3 * (1 + side) + row] = jnp.zeros((tile, LANES), jnp.bfloat16)

    @pl.when(jnp.logical_not(has_from))
    def _():
        @pl.loop(0, heads)
        def _(s):
            for t in (FAR, 3 + FAR, 6 + FAR):
                kr[s, t] = jnp.zeros((tile, LANES), jnp.bfloat16)

    pl.semaphore_wait(barrier, 2 * (count - 1))

    def k_cross(s):
        return remote(kr.at[s, OWN], kr.at[s, PART], kz_s.at[s], kz_r.at[s], partner)

    def k_across(s):
        target = jnp.where(has_outer, inner_tile, 0) + PART
        return remote(kr.at[s, OWN], kr.at[s, target], kz_s.at[s], kz_r.at[s], across)

    def k_relay(s):
        return remote(
            kr.at[s, outer_tile + PART], kr.at[s, PART],
            kf_s.at[s, outer_side, PART], kf_r.at[s, 1 - outer_side, PART], outer,
        )

    def k_far(s):
        return remote(kr.at[s, PART], kr.at[s, FAR], ky_s.at[s], ky_r.at[s], far_to)

    def k_far_outer(s):
        return remote(
            kr.at[s, outer_tile + PART], kr.at[s, outer_tile + FAR],
            kf_s.at[s, outer_side, FAR], kf_r.at[s, outer_side, FAR], far_to,
        )

    def k_inner(s, row):
        return remote(
            kr.at[s, row], kr.at[s, outer_tile + row],
            kf_s.at[s, inner_side, row], kf_r.at[s, 1 - inner_side, row], inner,
        )

    def k_frame(s, side):
        return remote(
            kr.at[s, OWN], kr.at[s, 3 * (2 - side)],
            kf_s.at[s, side, OWN], kf_r.at[s, 1 - side, OWN], sides[side][0],
        )

    def k_in(s, tile_index, side, row):
        return remote(
            kr.at[s, tile_index], kr.at[s, tile_index], kf_s.at[s, side, row], kf_r.at[s, side, row], inner,
        )

    def g_frame(s, side):
        return remote(
            gp.at[s, 3 * (1 + side)], gf.at[s, 1 - side, OWN],
            gf_s.at[s, side, OWN], gf_r.at[s, 1 - side, OWN], sides[side][0],
        )

    def g_inner(s, row):
        return remote(
            gp.at[s, inner_tile + row], gf.at[s, 1 - inner_side, row],
            gf_s.at[s, inner_side, row], gf_r.at[s, 1 - inner_side, row], inner,
        )

    def g_far_outer(s):
        return remote(
            gp.at[s, outer_tile + FAR], gf.at[s, outer_side, FAR],
            gf_s.at[s, outer_side, FAR], gf_r.at[s, outer_side, FAR], far_from,
        )

    def g_relay(s):
        return remote(
            gp.at[s, PART], gf.at[s, 1 - outer_side, PART],
            gf_s.at[s, outer_side, PART], gf_r.at[s, 1 - outer_side, PART], outer,
        )

    def g_in(s, side, row):
        return remote(
            gf.at[s, side, row], gf.at[s, side, row], gf_s.at[s, side, row], gf_r.at[s, side, row], inner,
        )

    def g_far(s):
        return remote(gp.at[s, FAR], gy.at[s], gy_s.at[s], gy_r.at[s], far_from)

    def g_cross(s):
        return remote(gp.at[s, PART], gz.at[s], gz_s.at[s], gz_r.at[s], partner)

    def g_across(s):
        return remote(gp.at[s, outer_tile + PART], gz.at[s], gz_s.at[s], gz_r.at[s], across)

    def each_side(fn):
        for side in range(2):
            @pl.when(sides[side][1])
            def _(side=side):
                fn(side)

    def when(cond, fn):
        @pl.when(cond)
        def _():
            fn()

    lane = lax.broadcasted_iota(jnp.int32, (2, 8, tile), 2)
    group = lax.broadcasted_iota(jnp.int32, (2, 8, tile), 0)
    cross_col = jnp.where(lax.rem(lane // TW, 2) != group, 1.0, 0.0)
    to_log2 = jnp.float32(LANES**-0.5 * LOG2E)

    def attend(s, tiles):
        head = meta[0, s]
        q = by_head[1, head]
        bias = cross_col * closed[2, s]
        low_limit = closed[0, s] + jnp.where(has_low, 0.0, NEG)
        high_limit = closed[0, s] + jnp.where(has_high, 0.0, NEG)
        far_limit = closed[1, s] + jnp.where(has_from, 0.0, NEG)
        stride, number = tiles

        def score(n, keys, limit, top):
            sc = dot(keys, q, 1, 1)
            if limit is not None:
                sc = (sc.reshape(tile // 16, 2, 8, tile) + limit).reshape(tile, tile)
            s_ref[n] = sc
            return jnp.maximum(top, jnp.max(sc.reshape(tile // 8, 8, tile), axis=0))

        def score_tile(n, top):
            t = n * stride
            limit = bias
            if t // 3:
                limit = limit + (low_limit, high_limit)[t // 3 - 1]
            if t % 3:
                limit = limit + (closed[1, s], far_limit)[t % 3 - 1]
            return score(n, kr[s, t], limit, top)

        top = score(number, by_head[3, head], None, jnp.full((8, tile), NEG, jnp.float32))
        for n in range(number):
            top = score_tile(n, top)
        top = jnp.max(top, axis=0, keepdims=True)

        def weigh(n, total):
            e = jnp.exp2((s_ref[n] - top) * to_log2)
            p_ref[n] = e.astype(jnp.bfloat16)
            return total + jnp.sum(e.reshape(tile // 8, 8, tile), axis=0)

        total = jnp.zeros((8, tile), jnp.float32)
        for n in range(number + 1):
            total = weigh(n, total)
        total = jnp.sum(total, axis=0, keepdims=True)
        inverse = jnp.transpose(jnp.broadcast_to(1.0 / total, (8, tile)))[:, :1]
        cot = (by_head[2, head].astype(jnp.float32) * inverse).astype(jnp.bfloat16)
        tvs[s] = dot(p_ref[number], cot, 1, 0)

        for n in range(number):
            t = n * stride
            grad = dot(p_ref[n], cot, 1, 0)
            if t < 3:
                ga[s, t] = grad
            else:
                gp[s, t] = grad.astype(jnp.bfloat16)

    def in_range(i, lo, hi, fn):
        if hi > lo:
            @pl.when((i >= lo) & (i < hi))
            def _():
                fn(i)

    def start_cross(s):
        in_range(s, 0, n_a, lambda s: k_across(s).start())
        in_range(s, n_a, n_rows, lambda s: k_cross(s).start())

    def start_frames(s):
        each_side(lambda side: k_frame(s, side).start())

    def pass_outer(s):
        k_cross(s).wait_recv()

        @pl.when(has_outer)
        def _():
            k_relay(s).start()
            when(has_to, lambda: k_far_outer(s).start())

    def pass_partner(s):
        when(has_outer, lambda: k_in(s, PART, outer_side, PART).wait_recv())
        when(has_to, lambda: k_far(s).start())
        k_inner(s, PART).start()

    def pass_partner_b(s):
        k_cross(s).wait_recv()
        when(has_to, lambda: k_far(s).start())

    def pass_far(s):
        @pl.when(has_from)
        def _():
            k_far(s).wait_recv()
            in_range(s, 0, n_a, lambda s: k_inner(s, FAR).start())

    def frames_in(s):
        each_side(lambda side: k_in(s, 3 * (1 + side), side, OWN).wait_recv())

    def compute_a(s):
        frames_in(s)
        k_in(s, inner_tile + PART, inner_side, PART).wait_recv()

        @pl.when(has_from)
        def _():
            k_in(s, inner_tile + FAR, inner_side, FAR).wait_recv()
            when(has_outer, lambda: k_in(s, outer_tile + FAR, outer_side, FAR).wait_recv())
        attend(s, (1, 9))

        @pl.when(has_from)
        def _():
            when(has_outer, lambda: g_far_outer(s).start())
            g_inner(s, FAR).start()
        g_inner(s, PART).start()
        each_side(lambda side: g_frame(s, side).start())

    def compute_b(s):
        attend(s, (1, 3))

    def compute_c(s):
        frames_in(s)
        attend(s, (3, 3))
        each_side(lambda side: g_frame(s, side).start())

    def add_in(s, side, row, into):
        g_in(s, side, row).wait_recv()
        ga[s, into] = ga[s, into] + gf[s, side, row].astype(jnp.float32)

    def add_frames(s):
        each_side(lambda side: add_in(s, side, OWN, OWN))

    def reduce_far(s):
        @pl.when(has_from)
        def _():
            in_range(s, 0, n_a, lambda s: add_in(s, inner_side, FAR, FAR))
            gp[s, FAR] = ga[s, FAR].astype(jnp.bfloat16)
            g_far(s).start()

    def reduce_partner(s):
        in_range(s, 0, n_a, lambda s: add_in(s, inner_side, PART, PART))

        @pl.when(has_to)
        def _():
            g_far(s).wait_recv()
            ga[s, PART] = ga[s, PART] + gy[s].astype(jnp.float32)
        gp[s, PART] = ga[s, PART].astype(jnp.bfloat16)

        def send_a(s):
            when(has_outer, lambda: g_relay(s).start())
            when(jnp.logical_not(has_outer), lambda: g_cross(s).start())
        in_range(s, 0, n_a, send_a)
        in_range(s, n_a, n_rows, lambda s: g_cross(s).start())

    def relay(s):
        @pl.when(has_outer)
        def _():
            g_in(s, outer_side, PART).wait_recv()
            ga[s, FAR] = gp[s, outer_tile + PART].astype(jnp.float32) + gf[s, outer_side, PART].astype(jnp.float32)
            when(has_to, lambda: add_in(s, outer_side, FAR, FAR))
            gp[s, outer_tile + PART] = ga[s, FAR].astype(jnp.bfloat16)
            g_across(s).start()

    def finish(s):
        in_range(s, 0, n_a, add_frames)
        in_range(s, n_rows, heads, add_frames)
        if n_rows:
            @pl.when(s < n_rows)
            def _():
                g_cross(s).wait_recv()
                ga[s, OWN] = ga[s, OWN] + gz[s].astype(jnp.float32)
        grad = ga[s, OWN].astype(jnp.bfloat16)
        vgs[s] = grad
        up_s[s] = dot(hid_t[...], grad, 1, 0)
        back[...] = back[...] + dot(grad, ui_wide[meta[0, s]], 1, 1)

    for s in map(jnp.int32, range(min(AHEAD, n_rows))):
        start_cross(s)

    @pl.loop(0, heads)
    def _(s):
        in_range(s, 0, n_a, start_frames)
        in_range(s, n_rows, heads, start_frames)

    depth = clean_ref.shape[1]
    rank = ui_ref.shape[0]
    copies = LANES // rank
    per = heads
    lane8 = lax.broadcasted_iota(jnp.int32, (1, copies, LANES), 2)
    row8 = lax.broadcasted_iota(jnp.int32, (1, copies, LANES), 1)
    pick = lane8 // rank == row8

    block = 512
    blocks = depth // block
    sketch_rows = SKETCH // LANES
    pieces = flat.shape[0] // sketch_rows

    def place_down(base, n, wide):
        kept = jnp.where(pick, wide.reshape(-1, copies, LANES), 0.0)
        flat[pl.ds(pl.multiple_of(base + n * (block // copies), 64), block // copies), :] = jnp.sum(kept, axis=1)

    def place_up(base, m, grad):
        for r in range(rank):
            flat[pl.ds(base + r * per + m, 1), :] = grad[r:r + 1, :]

    for n, ref in enumerate((q_ref, c_ref, tk_ref)):
        loads[n].wait()

        @pl.loop(0, heads)
        def _(j):
            by_head[n + 1, j] = ref[:, columns(j)]

    @pl.loop(0, heads)
    def _(j):
        ui_wide[j] = jnp.concatenate([ui_ref[:, columns(j)]] * copies, axis=0)

    back[...] = jnp.zeros_like(back)
    for n in range(3, 6):
        loads[n].wait()
    level = jnp.full((1, block), time_ref[0], jnp.int32).astype(jnp.float32) / 1000.0

    def mix(n, hid):
        cols = columns(n, block)
        mixed = (
            (1.0 - level) * clean_ref[:, cols].astype(jnp.float32)
            + level * noise_ref[:, cols].astype(jnp.float32)
        ).astype(jnp.bfloat16)
        mixed_t[n] = jnp.transpose(mixed)
        return hid + dot(di_ref[:, cols], mixed, 1, 1)

    hid_t[...] = lax.fori_loop(0, blocks, mix, jnp.zeros((rank, tile), jnp.float32)).astype(jnp.bfloat16)
    text_hid[...] = dot(dt_ref[...], text_ref[...], 1, 1)

    @pl.loop(0, pieces)
    def _(m):
        pos = lax.broadcasted_iota(jnp.int32, (sketch_rows, LANES), 0) * LANES
        pos = pos + lax.broadcasted_iota(jnp.int32, (sketch_rows, LANES), 1) + m * SKETCH
        bits = pos * 1103515245 + seed_ref[0] * 12345 + 1013904223
        bits = bits ^ (bits >> 16)
        bits = bits * 73244475
        bits = bits ^ (bits >> 16)
        signs[m] = (1 - 2 * ((bits >> 7) & 1)).astype(jnp.float32)

    def text_grads():
        th_hi, th_lo = split2(text_hid[...])

        def per_head(j, text_back):
            tv_hi, tv_lo = split2(tvs[meta[1, j]])
            place_up(960, j, dot(th_hi, tv_hi, 1, 0) + (dot(th_hi, tv_lo, 1, 0) + dot(th_lo, tv_hi, 1, 0)))
            cols = jnp.concatenate([ut_ref[:, columns(j)]] * copies, axis=0)
            return text_back + (dot(tv_hi, cols, 1, 1) + dot(tv_lo, cols, 1, 1))

        text_back = lax.fori_loop(0, heads, per_head, jnp.zeros((tile, LANES), jnp.float32))
        tb_hi, tb_lo = split2(text_back)

        @pl.loop(0, blocks)
        def _(n):
            text = text_ref[:, columns(n, block)]
            place_down(576, n, dot(text, tb_hi, 0, 0) + dot(text, tb_lo, 0, 0))

    @pl.loop(0, heads + 8)
    def _(i):
        in_range(i + AHEAD, 0, n_rows, start_cross)
        in_range(i - 8, 0, heads, finish)
        in_range(i, heads + 3, heads + 4, lambda i: text_grads())
        in_range(i - 6, 0, n_a, relay)
        in_range(i - 5, 0, n_rows, reduce_partner)
        in_range(i - 4, 0, n_rows, reduce_far)
        in_range(i - 3, n_rows, heads, compute_c)
        in_range(i - 3, n_a, n_rows, compute_b)
        in_range(i - 3, 0, n_a, compute_a)
        in_range(i - 2, 0, n_rows, pass_far)
        in_range(i - 1, 0, n_a, pass_partner)
        in_range(i, n_a, n_rows, pass_partner_b)
        in_range(i, 0, n_a, pass_outer)

    @pl.loop(0, heads)
    def _(j):
        slot = meta[1, j]
        vg_ref[:, columns(j)] = vgs[slot]
        place_up(384, j, up_s[slot])

    low_back = back[...].astype(jnp.bfloat16)

    @pl.loop(0, blocks)
    def _(n):
        place_down(0, n, dot(mixed_t[n], low_back, 1, 0))

    acc = flat[0:sketch_rows] * signs[0]
    for m in range(1, pieces):
        acc = acc + flat[m * sketch_rows:(m + 1) * sketch_rows] * signs[m]
    part[...] = (acc * (token_total * pieces) ** -0.5).reshape(count, sketch_rows // count, LANES)

    def send1(k):
        i = lax.rem(g + k, count)
        return remote(part.at[i], box1.at[g], a_s.at[0, k], a_r.at[0, g], in_ring(i))

    def send2(k):
        i = lax.rem(w + k, count)
        return remote(box2.at[w], box2.at[w], a_s.at[1, k], a_r.at[1, w], in_plane(i))

    def send3(k):
        i = lax.rem(g + k, count)
        return remote(out_ref.at[g], out_ref.at[g], a_s.at[2, k], a_r.at[2, g], in_ring(i))

    def recv(phase, dst, i):
        return remote(dst.at[i], dst.at[i], a_s.at[phase, 0], a_r.at[phase, i], in_ring(lax.rem(g + 1, count)))

    def phase(n, me, dst, send):
        @pl.loop(1, count)
        def _(k):
            send(k).start()

        @pl.loop(1, count)
        def _(k):
            recv(n, dst, lax.rem(me + k, count)).wait_recv()

    box1[g] = part[g]
    phase(0, g, box1, send1)
    box2[w] = jnp.sum(box1[...], axis=0)
    phase(1, w, box2, send2)
    out_ref[g] = jnp.sum(box2[...], axis=0)
    phase(2, g, out_ref, send3)

    @pl.loop(1, count)
    def _(k):
        send1(k).wait_send()
        send2(k).wait_send()
        send3(k).wait_send()

    @pl.loop(0, heads)
    def _(s):
        def sent_rows(s):
            k_cross(s).wait_send()
            g_cross(s).wait_send()
            when(has_to, lambda: k_far(s).wait_send())
            when(has_from, lambda: g_far(s).wait_send())

        def sent_own(s):
            each_side(lambda side: k_frame(s, side).wait_send())
            each_side(lambda side: g_frame(s, side).wait_send())

        def sent_a(s):
            sent_own(s)
            k_inner(s, PART).wait_send()
            g_inner(s, PART).wait_send()

            @pl.when(has_from)
            def _():
                k_inner(s, FAR).wait_send()
                g_inner(s, FAR).wait_send()
                when(has_outer, lambda: g_far_outer(s).wait_send())

            @pl.when(has_outer)
            def _():
                k_relay(s).wait_send()
                g_relay(s).wait_send()
                when(has_to, lambda: k_far_outer(s).wait_send())

        in_range(s, 0, n_rows, sent_rows)
        in_range(s, 0, n_a, sent_a)
        in_range(s, n_rows, heads, sent_own)


def attention(n_a, n_b, cid, frames, rows, *args):
    tile, width = args[4].shape
    depth = args[12].shape[1]
    rank = args[5].shape[0]
    lines = SKETCH // LANES
    heads = width // LANES
    vmem = pl.BlockSpec(memory_space=pltpu.VMEM)
    sem = pltpu.SemaphoreType.DMA
    bf, f32 = jnp.bfloat16, jnp.float32
    box = (tile, LANES)
    return pl.pallas_call(
        functools.partial(attention_kernel, n_a, n_b, heads, frames, rows, tile * frames * rows),
        out_shape=(jax.ShapeDtypeStruct((tile, width), bf), jax.ShapeDtypeStruct((16, lines // 16, LANES), f32)),
        in_specs=[pl.BlockSpec(memory_space=pltpu.SMEM)] * 4 + [vmem] * 5 + [pl.BlockSpec(memory_space=pl.ANY)] * 6,
        out_specs=(vmem, vmem),
        scratch_shapes=[
            pltpu.VMEM((tile, width), bf), pltpu.VMEM((tile, width), bf), pltpu.VMEM((tile, width), bf),
            pltpu.VMEM((tile, depth), bf), pltpu.VMEM((tile, depth), bf), pltpu.VMEM((tile, depth), bf),
            sem((6,)),
            pltpu.VMEM((depth // 512, 512, tile), bf),
            pltpu.VMEM((rank, tile), bf),
            pltpu.VMEM((rank, tile), f32),
            pltpu.VMEM((heads, LANES, LANES), bf),
            pltpu.VMEM((tile, LANES), f32),
            pltpu.VMEM((heads, rank, LANES), f32),
            pltpu.VMEM((9 * lines, LANES), f32),
            pltpu.VMEM((9, lines, LANES), f32),
            pltpu.VMEM((16, lines // 16, LANES), f32),
            pltpu.VMEM((16, lines // 16, LANES), f32),
            pltpu.VMEM((16, lines // 16, LANES), f32),
            sem((3, 16)), sem((3, 16)),
            pltpu.VMEM((4, heads) + box, bf),
            pltpu.VMEM((heads, 9) + box, bf),
            pltpu.VMEM((heads, 9) + box, bf),
            pltpu.VMEM((heads, 3) + box, f32),
            pltpu.VMEM((heads, 2, 3) + box, bf),
            pltpu.VMEM((heads,) + box, bf),
            pltpu.VMEM((heads,) + box, bf),
            pltpu.VMEM((heads,) + box, bf),
            pltpu.VMEM((heads,) + box, f32),
            pltpu.VMEM((10, tile, tile), f32),
            pltpu.VMEM((10, tile, tile), bf),
            sem((heads,)), sem((heads,)), sem((heads,)), sem((heads,)),
            sem((heads, 2, 3)), sem((heads, 2, 3)), sem((heads, 2, 3)), sem((heads, 2, 3)),
            sem((heads,)), sem((heads,)), sem((heads,)), sem((heads,)),
        ],
        compiler_params=pltpu.CompilerParams(
            collective_id=cid, has_side_effects=True, vmem_limit_bytes=56 << 20
        ),
    )(*args)


def split2(x):
    hi = x.astype(jnp.bfloat16)
    return hi, (x - hi.astype(jnp.float32)).astype(jnp.bfloat16)


VARIANTS = ((2, 2), (3, 2), (4, 2), (5, 2), (6, 3), (12, 0))


def plan_kernel(variants, heads, radii, choice, meta, closed):
    kinds = []
    counts = [jnp.int32(0)] * 4
    ranks = []
    for j in range(heads):
        far_f, far_r = radii[0, j] > 0, radii[1, j] > 0
        kind = jnp.where(far_r, jnp.where(far_f, 0, 1), jnp.where(far_f, 2, 3))
        kinds.append(kind)
        rank = jnp.int32(0)
        for t in range(4):
            rank = jnp.where(kind == t, counts[t], rank)
            counts[t] = counts[t] + jnp.where(kind == t, 1, 0)
        ranks.append(rank)
    pick = jnp.int32(len(variants) - 1)
    a, b = jnp.int32(variants[-1][0]), jnp.int32(variants[-1][1])
    for i in reversed(range(len(variants) - 1)):
        va, vb = variants[i]
        vc = heads - va - vb
        fits = (counts[0] <= va) & (counts[0] + counts[1] <= va + vb) & (counts[0] + counts[2] <= va + vc)
        pick = jnp.where(fits, i, pick)
        a, b = jnp.where(fits, va, a), jnp.where(fits, vb, b)
    c = heads - a - b
    over_b = jnp.maximum(counts[1] - b, 0)
    over_c = jnp.maximum(counts[2] - c, 0)
    spare_a = a - counts[0] - over_b - over_c
    spare_b = b - (counts[1] - over_b)
    choice[0] = pick
    for j in range(heads):
        kind, rank = kinds[j], ranks[j]
        slot_b = jnp.where(rank < over_b, counts[0] + rank, a + rank - over_b)
        slot_c = jnp.where(rank < over_c, counts[0] + over_b + rank, heads - counts[2] + rank)
        left = rank - spare_a - spare_b
        slot_d = jnp.where(
            rank < spare_a,
            counts[0] + over_b + over_c + rank,
            a + b + left,
        )
        slot = jnp.where(kind == 0, rank, jnp.where(kind == 1, slot_b, jnp.where(kind == 2, slot_c, slot_d)))
        meta[0, slot] = j
        meta[1, j] = slot
        for r in range(3):
            closed[r, slot] = jnp.where(radii[r, j] > 0, 0.0, NEG)


def plan(radii):
    heads = radii.shape[1]
    smem = pl.BlockSpec(memory_space=pltpu.SMEM)
    return pl.pallas_call(
        functools.partial(plan_kernel, VARIANTS, heads),
        out_shape=(
            jax.ShapeDtypeStruct((1,), jnp.int32),
            jax.ShapeDtypeStruct((2, heads), jnp.int32),
            jax.ShapeDtypeStruct((3, heads), jnp.float32),
        ),
        in_specs=[smem],
        out_specs=(smem, smem, smem),
    )(radii)


def per_device(
    clean_latents, gaussian_noise, text_states, queries, key_states, cotangent, text_keys,
    window_radii, timestep, sketch_seed, down_image, up_image, down_text, up_text,
):
    width = queries.shape[-1]
    depth = clean_latents.shape[-1]
    frames, rows = lax.axis_size("tm"), lax.axis_size("height")
    choice, meta, closed = plan(window_radii.T)
    branches = [
        functools.partial(attention, a, b, i + 1, frames, rows) for i, (a, b) in enumerate(VARIANTS)
    ]
    operands = (
        meta, closed, timestep, sketch_seed,
        key_states.reshape(-1, width), up_image, up_text, down_image.T, down_text.T,
        queries.reshape(-1, width), cotangent.reshape(-1, width), text_keys,
        clean_latents.reshape(-1, depth), gaussian_noise.reshape(-1, depth), text_states,
    )
    if len(branches) == 1:
        vg, sk = branches[0](*operands)
    else:
        vg, sk = lax.switch(choice[0], branches, *operands)
    return vg.reshape(queries.shape), sk.reshape(-1)


def solution(mesh):
    block = P("tm", "height", None, None)
    return jax.shard_map(
        per_device,
        mesh=mesh,
        in_specs=(block, block, P(), block, block, block) + (P(),) * 8,
        out_specs=(block, P()),
        check_vma=False,
    )
```

```python
import functools

import jax
import jax.numpy as jnp
from jax import lax
from jax.experimental import pallas as pl
from jax.experimental.pallas import tpu as pltpu
from jax.sharding import PartitionSpec as P

MESH = pl.DeviceIdType.MESH
TW = 8
LANES = 128
SKETCH = 16384
NEG = -1e30
LOG2E = 1.4426950408889634
OWN, PART, FAR = 0, 1, 2
AHEAD = 1


def dot(a, b, ca, cb):
    return lax.dot_general(a, b, (((ca,), (cb,)), ((), ())), preferred_element_type=jnp.float32)


def remote(src, dst, ssem, rsem, device):
    return pltpu.make_async_remote_copy(
        src_ref=src, dst_ref=dst, send_sem=ssem, recv_sem=rsem, device_id=device, device_id_type=MESH
    )


def attention_kernel(
    n_a, n_b, heads, frames, rows, token_total,
    meta, closed, time_ref, seed_ref, k_ref, ui_ref, ut_ref, di_ref, dt_ref,
    q_hbm, c_hbm, tk_hbm, clean_hbm, noise_hbm, text_hbm, vg_ref, out_ref,
    q_ref, c_ref, tk_ref, clean_ref, noise_ref, text_ref, l_sem,
    mixed_t, hid_t, text_hid, ui_wide, back, up_s, flat, signs, part, box1, box2, a_s, a_r,
    by_head, kr, gp, ga, gf, gy, gz, vgs, tvs, s_ref, p_ref,
    kz_s, kz_r, ky_s, ky_r, kf_s, kf_r, gf_s, gf_r, gy_s, gy_r, gz_s, gz_r,
):
    n_rows = n_a + n_b
    tile = k_ref.shape[0]
    f = lax.axis_index("tm")
    h = lax.axis_index("height")
    even = lax.rem(h, 2) == 0
    partner = (f, h + 1 - 2 * lax.rem(h, 2))
    step = 2 - 4 * lax.rem(h, 2)
    has_to = (h + step >= 0) & (h + step < rows)
    has_from = (h - step >= 0) & (h - step < rows)
    far_to = (f, jnp.where(has_to, h + step, h))
    far_from = (f, jnp.where(has_from, h - step, h))
    has_low = f > 0
    has_high = f < frames - 1
    low = (jnp.maximum(f - 1, 0), h)
    high = (jnp.minimum(f + 1, frames - 1), h)
    sides = ((low, has_low), (high, has_high))
    odd = lax.rem(f, 2)
    has_outer = jnp.where(odd == 1, f < frames - 1, f > 0)
    outer_f = jnp.where(has_outer, f - 1 + 2 * odd, f)
    outer = (outer_f, h)
    across = (outer_f, partner[1])
    inner = (f + 1 - 2 * odd, h)
    outer_side, inner_side = odd, 1 - odd
    outer_tile = 3 * (1 + odd)
    inner_tile = 3 * (2 - odd)

    g = 2 * f + lax.rem(h, 2)
    w = h // 2
    count = 16

    def in_ring(i):
        return (i // 2, 2 * w + lax.rem(i, 2))

    def in_plane(i):
        return (f, 2 * i + lax.rem(h, 2))

    barrier = pltpu.get_barrier_semaphore()

    @pl.loop(1, count)
    def _(k):
        pl.semaphore_signal(barrier, inc=1, device_id=in_ring(lax.rem(g + k, count)), device_id_type=MESH)
        pl.semaphore_signal(barrier, inc=1, device_id=in_plane(lax.rem(w + k, count)), device_id_type=MESH)

    loads = [
        pltpu.make_async_copy(src, dst, l_sem.at[n])
        for n, (src, dst) in enumerate((
            (q_hbm, q_ref), (c_hbm, c_ref), (tk_hbm, tk_ref),
            (clean_hbm, clean_ref), (noise_hbm, noise_ref), (text_hbm, text_ref),
        ))
    ]
    for load in loads:
        load.start()

    def columns(j, size=LANES):
        return pl.ds(pl.multiple_of(j * size, size), size)

    @pl.loop(0, heads)
    def _(j):
        by_head[0, j] = k_ref[:, columns(j)]

    @pl.loop(0, heads)
    def _(s):
        kr[s, 0] = by_head[0, meta[0, s]]

    for side, exists in enumerate((has_low, has_high)):
        @pl.when(jnp.logical_not(exists))
        def _(side=side):
            @pl.loop(0, heads)
            def _(s):
                for row in range(3):
                    kr[s, 3 * (1 + side) + row] = jnp.zeros((tile, LANES), jnp.bfloat16)

    @pl.when(jnp.logical_not(has_from))
    def _():
        @pl.loop(0, heads)
        def _(s):
            for t in (FAR, 3 + FAR, 6 + FAR):
                kr[s, t] = jnp.zeros((tile, LANES), jnp.bfloat16)

    pl.semaphore_wait(barrier, 2 * (count - 1))

    def k_cross(s):
        return remote(kr.at[s, OWN], kr.at[s, PART], kz_s.at[s], kz_r.at[s], partner)

    def k_across(s):
        target = jnp.where(has_outer, inner_tile, 0) + PART
        return remote(kr.at[s, OWN], kr.at[s, target], kz_s.at[s], kz_r.at[s], across)

    def k_relay(s):
        return remote(
            kr.at[s, outer_tile + PART], kr.at[s, PART],
            kf_s.at[s, outer_side, PART], kf_r.at[s, 1 - outer_side, PART], outer,
        )

    def k_far(s):
        return remote(kr.at[s, PART], kr.at[s, FAR], ky_s.at[s], ky_r.at[s], far_to)

    def k_far_outer(s):
        return remote(
            kr.at[s, outer_tile + PART], kr.at[s, outer_tile + FAR],
            kf_s.at[s, outer_side, FAR], kf_r.at[s, outer_side, FAR], far_to,
        )

    def k_inner(s, row):
        return remote(
            kr.at[s, row], kr.at[s, outer_tile + row],
            kf_s.at[s, inner_side, row], kf_r.at[s, 1 - inner_side, row], inner,
        )

    def k_frame(s, side):
        return remote(
            kr.at[s, OWN], kr.at[s, 3 * (2 - side)],
            kf_s.at[s, side, OWN], kf_r.at[s, 1 - side, OWN], sides[side][0],
        )

    def k_in(s, tile_index, side, row):
        return remote(
            kr.at[s, tile_index], kr.at[s, tile_index], kf_s.at[s, side, row], kf_r.at[s, side, row], inner,
        )

    def g_frame(s, side):
        return remote(
            gp.at[s, 3 * (1 + side)], gf.at[s, 1 - side, OWN],
            gf_s.at[s, side, OWN], gf_r.at[s, 1 - side, OWN], sides[side][0],
        )

    def g_inner(s, row):
        return remote(
            gp.at[s, inner_tile + row], gf.at[s, 1 - inner_side, row],
            gf_s.at[s, inner_side, row], gf_r.at[s, 1 - inner_side, row], inner,
        )

    def g_far_outer(s):
        return remote(
            gp.at[s, outer_tile + FAR], gf.at[s, outer_side, FAR],
            gf_s.at[s, outer_side, FAR], gf_r.at[s, outer_side, FAR], far_from,
        )

    def g_relay(s):
        return remote(
            gp.at[s, PART], gf.at[s, 1 - outer_side, PART],
            gf_s.at[s, outer_side, PART], gf_r.at[s, 1 - outer_side, PART], outer,
        )

    def g_in(s, side, row):
        return remote(
            gf.at[s, side, row], gf.at[s, side, row], gf_s.at[s, side, row], gf_r.at[s, side, row], inner,
        )

    def g_far(s):
        return remote(gp.at[s, FAR], gy.at[s], gy_s.at[s], gy_r.at[s], far_from)

    def g_cross(s):
        return remote(gp.at[s, PART], gz.at[s], gz_s.at[s], gz_r.at[s], partner)

    def g_across(s):
        return remote(gp.at[s, outer_tile + PART], gz.at[s], gz_s.at[s], gz_r.at[s], across)

    def each_side(fn):
        for side in range(2):
            @pl.when(sides[side][1])
            def _(side=side):
                fn(side)

    def when(cond, fn):
        @pl.when(cond)
        def _():
            fn()

    lane = lax.broadcasted_iota(jnp.int32, (2, 8, tile), 2)
    group = lax.broadcasted_iota(jnp.int32, (2, 8, tile), 0)
    cross_col = jnp.where(lax.rem(lane // TW, 2) != group, 1.0, 0.0)
    to_log2 = jnp.float32(LANES**-0.5 * LOG2E)

    def attend(s, tiles):
        head = meta[0, s]
        q = by_head[1, head]
        bias = cross_col * closed[2, s]
        low_limit = closed[0, s] + jnp.where(has_low, 0.0, NEG)
        high_limit = closed[0, s] + jnp.where(has_high, 0.0, NEG)
        far_limit = closed[1, s] + jnp.where(has_from, 0.0, NEG)
        stride, number = tiles

        def score(n, keys, limit, top):
            sc = dot(keys, q, 1, 1)
            if limit is not None:
                sc = (sc.reshape(tile // 16, 2, 8, tile) + limit).reshape(tile, tile)
            s_ref[n] = sc
            return jnp.maximum(top, jnp.max(sc.reshape(tile // 8, 8, tile), axis=0))

        def score_tile(n, top):
            t = n * stride
            limit = bias
            if t // 3:
                limit = limit + (low_limit, high_limit)[t // 3 - 1]
            if t % 3:
                limit = limit + (closed[1, s], far_limit)[t % 3 - 1]
            return score(n, kr[s, t], limit, top)

        top = score(number, by_head[3, head], None, jnp.full((8, tile), NEG, jnp.float32))
        for n in range(number):
            top = score_tile(n, top)
        top = jnp.max(top, axis=0, keepdims=True)

        def weigh(n, total):
            e = jnp.exp2((s_ref[n] - top) * to_log2)
            p_ref[n] = e.astype(jnp.bfloat16)
            return total + jnp.sum(e.reshape(tile // 8, 8, tile), axis=0)

        total = jnp.zeros((8, tile), jnp.float32)
        for n in range(number + 1):
            total = weigh(n, total)
        total = jnp.sum(total, axis=0, keepdims=True)
        inverse = jnp.transpose(jnp.broadcast_to(1.0 / total, (8, tile)))[:, :1]
        cot = (by_head[2, head].astype(jnp.float32) * inverse).astype(jnp.bfloat16)
        tvs[s] = dot(p_ref[number], cot, 1, 0)

        for n in range(number):
            t = n * stride
            grad = dot(p_ref[n], cot, 1, 0)
            if t < 3:
                ga[s, t] = grad
            else:
                gp[s, t] = grad.astype(jnp.bfloat16)

    def in_range(i, lo, hi, fn):
        if hi > lo:
            @pl.when((i >= lo) & (i < hi))
            def _():
                fn(i)

    def start_cross(s):
        in_range(s, 0, n_a, lambda s: k_across(s).start())
        in_range(s, n_a, n_rows, lambda s: k_cross(s).start())

    def start_frames(s):
        each_side(lambda side: k_frame(s, side).start())

    def pass_outer(s):
        k_cross(s).wait_recv()

        @pl.when(has_outer)
        def _():
            k_relay(s).start()
            when(has_to, lambda: k_far_outer(s).start())

    def pass_partner(s):
        when(has_outer, lambda: k_in(s, PART, outer_side, PART).wait_recv())
        when(has_to, lambda: k_far(s).start())
        k_inner(s, PART).start()

    def pass_partner_b(s):
        k_cross(s).wait_recv()
        when(has_to, lambda: k_far(s).start())

    def pass_far(s):
        @pl.when(has_from)
        def _():
            k_far(s).wait_recv()
            in_range(s, 0, n_a, lambda s: k_inner(s, FAR).start())

    def frames_in(s):
        each_side(lambda side: k_in(s, 3 * (1 + side), side, OWN).wait_recv())

    def compute_a(s):
        frames_in(s)
        k_in(s, inner_tile + PART, inner_side, PART).wait_recv()

        @pl.when(has_from)
        def _():
            k_in(s, inner_tile + FAR, inner_side, FAR).wait_recv()
            when(has_outer, lambda: k_in(s, outer_tile + FAR, outer_side, FAR).wait_recv())
        attend(s, (1, 9))

        @pl.when(has_from)
        def _():
            when(has_outer, lambda: g_far_outer(s).start())
            g_inner(s, FAR).start()
        g_inner(s, PART).start()
        each_side(lambda side: g_frame(s, side).start())

    def compute_b(s):
        attend(s, (1, 3))

    def compute_c(s):
        frames_in(s)
        attend(s, (3, 3))
        each_side(lambda side: g_frame(s, side).start())

    def add_in(s, side, row, into):
        g_in(s, side, row).wait_recv()
        ga[s, into] = ga[s, into] + gf[s, side, row].astype(jnp.float32)

    def add_frames(s):
        each_side(lambda side: add_in(s, side, OWN, OWN))

    def reduce_far(s):
        @pl.when(has_from)
        def _():
            in_range(s, 0, n_a, lambda s: add_in(s, inner_side, FAR, FAR))
            gp[s, FAR] = ga[s, FAR].astype(jnp.bfloat16)
            g_far(s).start()

    def reduce_partner(s):
        in_range(s, 0, n_a, lambda s: add_in(s, inner_side, PART, PART))

        @pl.when(has_to)
        def _():
            g_far(s).wait_recv()
            ga[s, PART] = ga[s, PART] + gy[s].astype(jnp.float32)
        gp[s, PART] = ga[s, PART].astype(jnp.bfloat16)

        def send_a(s):
            when(has_outer, lambda: g_relay(s).start())
            when(jnp.logical_not(has_outer), lambda: g_cross(s).start())
        in_range(s, 0, n_a, send_a)
        in_range(s, n_a, n_rows, lambda s: g_cross(s).start())

    def relay(s):
        @pl.when(has_outer)
        def _():
            g_in(s, outer_side, PART).wait_recv()
            ga[s, FAR] = gp[s, outer_tile + PART].astype(jnp.float32) + gf[s, outer_side, PART].astype(jnp.float32)
            when(has_to, lambda: add_in(s, outer_side, FAR, FAR))
            gp[s, outer_tile + PART] = ga[s, FAR].astype(jnp.bfloat16)
            g_across(s).start()

    def finish(s):
        in_range(s, 0, n_a, add_frames)
        in_range(s, n_rows, heads, add_frames)
        if n_rows:
            @pl.when(s < n_rows)
            def _():
                g_cross(s).wait_recv()
                ga[s, OWN] = ga[s, OWN] + gz[s].astype(jnp.float32)
        grad = ga[s, OWN].astype(jnp.bfloat16)
        vgs[s] = grad
        up_s[s] = dot(hid_t[...], grad, 1, 0)
        back[...] = back[...] + dot(grad, ui_wide[meta[0, s]], 1, 1)

    for s in map(jnp.int32, range(min(AHEAD, n_rows))):
        start_cross(s)

    for s in map(jnp.int32, range(3)):
        in_range(s, n_rows, heads, start_frames)

    depth = clean_ref.shape[1]
    rank = ui_ref.shape[0]
    copies = LANES // rank
    per = heads
    lane8 = lax.broadcasted_iota(jnp.int32, (1, copies, LANES), 2)
    row8 = lax.broadcasted_iota(jnp.int32, (1, copies, LANES), 1)
    pick = lane8 // rank == row8

    block = 512
    blocks = depth // block
    sketch_rows = SKETCH // LANES
    pieces = flat.shape[0] // sketch_rows

    def place_down(base, n, wide):
        kept = jnp.where(pick, wide.reshape(-1, copies, LANES), 0.0)
        flat[pl.ds(pl.multiple_of(base + n * (block // copies), 64), block // copies), :] = jnp.sum(kept, axis=1)

    def place_up(base, m, grad):
        for r in range(rank):
            flat[pl.ds(base + r * per + m, 1), :] = grad[r:r + 1, :]

    for n, ref in enumerate((q_ref, c_ref, tk_ref)):
        loads[n].wait()

        @pl.loop(0, heads)
        def _(j):
            by_head[n + 1, j] = ref[:, columns(j)]

    @pl.loop(0, heads)
    def _(j):
        ui_wide[j] = jnp.concatenate([ui_ref[:, columns(j)]] * copies, axis=0)

    back[...] = jnp.zeros_like(back)
    for n in range(3, 6):
        loads[n].wait()
    level = jnp.full((1, block), time_ref[0], jnp.int32).astype(jnp.float32) / 1000.0

    def mix(n, hid):
        cols = columns(n, block)
        mixed = (
            (1.0 - level) * clean_ref[:, cols].astype(jnp.float32)
            + level * noise_ref[:, cols].astype(jnp.float32)
        ).astype(jnp.bfloat16)
        mixed_t[n] = jnp.transpose(mixed)
        return hid + dot(di_ref[:, cols], mixed, 1, 1)

    hid_t[...] = lax.fori_loop(0, blocks, mix, jnp.zeros((rank, tile), jnp.float32)).astype(jnp.bfloat16)
    text_hid[...] = dot(dt_ref[...], text_ref[...], 1, 1)

    @pl.loop(0, pieces)
    def _(m):
        pos = lax.broadcasted_iota(jnp.int32, (sketch_rows, LANES), 0) * LANES
        pos = pos + lax.broadcasted_iota(jnp.int32, (sketch_rows, LANES), 1) + m * SKETCH
        bits = pos * 1103515245 + seed_ref[0] * 12345 + 1013904223
        bits = bits ^ (bits >> 16)
        bits = bits * 73244475
        bits = bits ^ (bits >> 16)
        signs[m] = (1 - 2 * ((bits >> 7) & 1)).astype(jnp.float32)

    def text_grads():
        th_hi, th_lo = split2(text_hid[...])

        def per_head(j, text_back):
            tv_hi, tv_lo = split2(tvs[meta[1, j]])
            place_up(960, j, dot(th_hi, tv_hi, 1, 0) + (dot(th_hi, tv_lo, 1, 0) + dot(th_lo, tv_hi, 1, 0)))
            cols = jnp.concatenate([ut_ref[:, columns(j)]] * copies, axis=0)
            return text_back + (dot(tv_hi, cols, 1, 1) + dot(tv_lo, cols, 1, 1))

        text_back = lax.fori_loop(0, heads, per_head, jnp.zeros((tile, LANES), jnp.float32))
        tb_hi, tb_lo = split2(text_back)

        @pl.loop(0, blocks)
        def _(n):
            text = text_ref[:, columns(n, block)]
            place_down(576, n, dot(text, tb_hi, 0, 0) + dot(text, tb_lo, 0, 0))

    @pl.loop(0, heads + 8)
    def _(i):
        in_range(i + AHEAD, 0, n_rows, start_cross)
        in_range(i, 0, n_a, start_frames)
        in_range(i + 3, max(n_rows, 3), heads, start_frames)
        in_range(i - 8, 0, heads, finish)
        in_range(i, heads + 3, heads + 4, lambda i: text_grads())
        in_range(i - 6, 0, n_a, relay)
        in_range(i - 5, 0, n_rows, reduce_partner)
        in_range(i - 4, 0, n_rows, reduce_far)
        in_range(i - 3, n_rows, heads, compute_c)
        in_range(i - 3, n_a, n_rows, compute_b)
        in_range(i - 3, 0, n_a, compute_a)
        in_range(i - 2, 0, n_rows, pass_far)
        in_range(i - 1, 0, n_a, pass_partner)
        in_range(i, n_a, n_rows, pass_partner_b)
        in_range(i, 0, n_a, pass_outer)

    @pl.loop(0, heads)
    def _(j):
        slot = meta[1, j]
        vg_ref[:, columns(j)] = vgs[slot]
        place_up(384, j, up_s[slot])

    low_back = back[...].astype(jnp.bfloat16)

    @pl.loop(0, blocks)
    def _(n):
        place_down(0, n, dot(mixed_t[n], low_back, 1, 0))

    acc = flat[0:sketch_rows] * signs[0]
    for m in range(1, pieces):
        acc = acc + flat[m * sketch_rows:(m + 1) * sketch_rows] * signs[m]
    part[...] = (acc * (token_total * pieces) ** -0.5).reshape(count, sketch_rows // count, LANES)

    def send1(k):
        i = lax.rem(g + k, count)
        return remote(part.at[i], box1.at[g], a_s.at[0, k], a_r.at[0, g], in_ring(i))

    def send2(k):
        i = lax.rem(w + k, count)
        return remote(box2.at[w], box2.at[w], a_s.at[1, k], a_r.at[1, w], in_plane(i))

    def send3(k):
        i = lax.rem(g + k, count)
        return remote(out_ref.at[g], out_ref.at[g], a_s.at[2, k], a_r.at[2, g], in_ring(i))

    def recv(phase, dst, i):
        return remote(dst.at[i], dst.at[i], a_s.at[phase, 0], a_r.at[phase, i], in_ring(lax.rem(g + 1, count)))

    def phase(n, me, dst, send):
        @pl.loop(1, count)
        def _(k):
            send(k).start()

        @pl.loop(1, count)
        def _(k):
            recv(n, dst, lax.rem(me + k, count)).wait_recv()

    box1[g] = part[g]
    phase(0, g, box1, send1)
    box2[w] = jnp.sum(box1[...], axis=0)
    phase(1, w, box2, send2)
    out_ref[g] = jnp.sum(box2[...], axis=0)
    phase(2, g, out_ref, send3)

    @pl.loop(1, count)
    def _(k):
        send1(k).wait_send()
        send2(k).wait_send()
        send3(k).wait_send()

    @pl.loop(0, heads)
    def _(s):
        def sent_rows(s):
            k_cross(s).wait_send()
            g_cross(s).wait_send()
            when(has_to, lambda: k_far(s).wait_send())
            when(has_from, lambda: g_far(s).wait_send())

        def sent_own(s):
            each_side(lambda side: k_frame(s, side).wait_send())
            each_side(lambda side: g_frame(s, side).wait_send())

        def sent_a(s):
            sent_own(s)
            k_inner(s, PART).wait_send()
            g_inner(s, PART).wait_send()

            @pl.when(has_from)
            def _():
                k_inner(s, FAR).wait_send()
                g_inner(s, FAR).wait_send()
                when(has_outer, lambda: g_far_outer(s).wait_send())

            @pl.when(has_outer)
            def _():
                k_relay(s).wait_send()
                g_relay(s).wait_send()
                when(has_to, lambda: k_far_outer(s).wait_send())

        in_range(s, 0, n_rows, sent_rows)
        in_range(s, 0, n_a, sent_a)
        in_range(s, n_rows, heads, sent_own)


def attention(n_a, n_b, cid, frames, rows, *args):
    tile, width = args[4].shape
    depth = args[12].shape[1]
    rank = args[5].shape[0]
    lines = SKETCH // LANES
    heads = width // LANES
    vmem = pl.BlockSpec(memory_space=pltpu.VMEM)
    sem = pltpu.SemaphoreType.DMA
    bf, f32 = jnp.bfloat16, jnp.float32
    box = (tile, LANES)
    return pl.pallas_call(
        functools.partial(attention_kernel, n_a, n_b, heads, frames, rows, tile * frames * rows),
        out_shape=(jax.ShapeDtypeStruct((tile, width), bf), jax.ShapeDtypeStruct((16, lines // 16, LANES), f32)),
        in_specs=[pl.BlockSpec(memory_space=pltpu.SMEM)] * 4 + [vmem] * 5 + [pl.BlockSpec(memory_space=pl.ANY)] * 6,
        out_specs=(vmem, vmem),
        scratch_shapes=[
            pltpu.VMEM((tile, width), bf), pltpu.VMEM((tile, width), bf), pltpu.VMEM((tile, width), bf),
            pltpu.VMEM((tile, depth), bf), pltpu.VMEM((tile, depth), bf), pltpu.VMEM((tile, depth), bf),
            sem((6,)),
            pltpu.VMEM((depth // 512, 512, tile), bf),
            pltpu.VMEM((rank, tile), bf),
            pltpu.VMEM((rank, tile), f32),
            pltpu.VMEM((heads, LANES, LANES), bf),
            pltpu.VMEM((tile, LANES), f32),
            pltpu.VMEM((heads, rank, LANES), f32),
            pltpu.VMEM((9 * lines, LANES), f32),
            pltpu.VMEM((9, lines, LANES), f32),
            pltpu.VMEM((16, lines // 16, LANES), f32),
            pltpu.VMEM((16, lines // 16, LANES), f32),
            pltpu.VMEM((16, lines // 16, LANES), f32),
            sem((3, 16)), sem((3, 16)),
            pltpu.VMEM((4, heads) + box, bf),
            pltpu.VMEM((heads, 9) + box, bf),
            pltpu.VMEM((heads, 9) + box, bf),
            pltpu.VMEM((heads, 3) + box, f32),
            pltpu.VMEM((heads, 2, 3) + box, bf),
            pltpu.VMEM((heads,) + box, bf),
            pltpu.VMEM((heads,) + box, bf),
            pltpu.VMEM((heads,) + box, bf),
            pltpu.VMEM((heads,) + box, f32),
            pltpu.VMEM((10, tile, tile), f32),
            pltpu.VMEM((10, tile, tile), bf),
            sem((heads,)), sem((heads,)), sem((heads,)), sem((heads,)),
            sem((heads, 2, 3)), sem((heads, 2, 3)), sem((heads, 2, 3)), sem((heads, 2, 3)),
            sem((heads,)), sem((heads,)), sem((heads,)), sem((heads,)),
        ],
        compiler_params=pltpu.CompilerParams(
            collective_id=cid, has_side_effects=True, vmem_limit_bytes=56 << 20
        ),
    )(*args)


def split2(x):
    hi = x.astype(jnp.bfloat16)
    return hi, (x - hi.astype(jnp.float32)).astype(jnp.bfloat16)


VARIANTS = ((2, 2), (3, 2), (4, 2), (5, 2), (6, 3), (12, 0))


def plan_kernel(variants, heads, radii, choice, meta, closed):
    kinds = []
    counts = [jnp.int32(0)] * 4
    ranks = []
    for j in range(heads):
        far_f, far_r = radii[0, j] > 0, radii[1, j] > 0
        kind = jnp.where(far_r, jnp.where(far_f, 0, 1), jnp.where(far_f, 2, 3))
        kinds.append(kind)
        rank = jnp.int32(0)
        for t in range(4):
            rank = jnp.where(kind == t, counts[t], rank)
            counts[t] = counts[t] + jnp.where(kind == t, 1, 0)
        ranks.append(rank)
    pick = jnp.int32(len(variants) - 1)
    a, b = jnp.int32(variants[-1][0]), jnp.int32(variants[-1][1])
    for i in reversed(range(len(variants) - 1)):
        va, vb = variants[i]
        vc = heads - va - vb
        fits = (counts[0] <= va) & (counts[0] + counts[1] <= va + vb) & (counts[0] + counts[2] <= va + vc)
        pick = jnp.where(fits, i, pick)
        a, b = jnp.where(fits, va, a), jnp.where(fits, vb, b)
    c = heads - a - b
    over_b = jnp.maximum(counts[1] - b, 0)
    over_c = jnp.maximum(counts[2] - c, 0)
    spare_a = a - counts[0] - over_b - over_c
    spare_b = b - (counts[1] - over_b)
    choice[0] = pick
    for j in range(heads):
        kind, rank = kinds[j], ranks[j]
        slot_b = jnp.where(rank < over_b, counts[0] + rank, a + rank - over_b)
        slot_c = jnp.where(rank < over_c, counts[0] + over_b + rank, heads - counts[2] + rank)
        left = rank - spare_a - spare_b
        slot_d = jnp.where(
            rank < spare_a,
            counts[0] + over_b + over_c + rank,
            a + b + left,
        )
        slot = jnp.where(kind == 0, rank, jnp.where(kind == 1, slot_b, jnp.where(kind == 2, slot_c, slot_d)))
        meta[0, slot] = j
        meta[1, j] = slot
        for r in range(3):
            closed[r, slot] = jnp.where(radii[r, j] > 0, 0.0, NEG)


def plan(radii):
    heads = radii.shape[1]
    smem = pl.BlockSpec(memory_space=pltpu.SMEM)
    return pl.pallas_call(
        functools.partial(plan_kernel, VARIANTS, heads),
        out_shape=(
            jax.ShapeDtypeStruct((1,), jnp.int32),
            jax.ShapeDtypeStruct((2, heads), jnp.int32),
            jax.ShapeDtypeStruct((3, heads), jnp.float32),
        ),
        in_specs=[smem],
        out_specs=(smem, smem, smem),
    )(radii)


def per_device(
    clean_latents, gaussian_noise, text_states, queries, key_states, cotangent, text_keys,
    window_radii, timestep, sketch_seed, down_image, up_image, down_text, up_text,
):
    width = queries.shape[-1]
    depth = clean_latents.shape[-1]
    frames, rows = lax.axis_size("tm"), lax.axis_size("height")
    choice, meta, closed = plan(window_radii.T)
    branches = [
        functools.partial(attention, a, b, i + 1, frames, rows) for i, (a, b) in enumerate(VARIANTS)
    ]
    operands = (
        meta, closed, timestep, sketch_seed,
        key_states.reshape(-1, width), up_image, up_text, down_image.T, down_text.T,
        queries.reshape(-1, width), cotangent.reshape(-1, width), text_keys,
        clean_latents.reshape(-1, depth), gaussian_noise.reshape(-1, depth), text_states,
    )
    if len(branches) == 1:
        vg, sk = branches[0](*operands)
    else:
        vg, sk = lax.switch(choice[0], branches, *operands)
    return vg.reshape(queries.shape), sk.reshape(-1)


def solution(mesh):
    block = P("tm", "height", None, None)
    return jax.shard_map(
        per_device,
        mesh=mesh,
        in_specs=(block, block, P(), block, block, block) + (P(),) * 8,
        out_specs=(block, P()),
        check_vma=False,
    )
```
